256 devices in a mesh: dp: 16 (over x, y), expert: 16 (over z, core).
Axes of the slice: x: 4, y: 4, z: 8, core: 2. Of those that a mesh axis runs over, the one named last changes fastest.
Arguments:
- tokens: bfloat16 [16384, 2048], P(('dp', 'expert')), may hold values from -6 to 6
- cotangent: bfloat16 [16384, 2048], P(('dp', 'expert')), may hold values from -6 to 6
- expert_ids: int32 [16384, 8], P(('dp', 'expert')), may hold values from 0 to 15, all different within a row
- gate_probs: float32 [16384, 8], P(('dp', 'expert')), may hold values from 0.05 to 0.5
- held_before: int32 [16], replicated, may hold values from 0 to 15, each once
- swap_flags: int32 [8], replicated, may hold values from 0 to 1, as said below
- weights: bfloat16 [16, 2048, 3, 384], P('expert'), may hold values from -0.125 to 0.125
Outputs:
- mixed: bfloat16 [16384, 2048], P(('dp', 'expert'))
- token_grads: bfloat16 [16384, 2048], P(('dp', 'expert'))
- gate_grads: float32 [16384, 8], P(('dp', 'expert'))
- weight_grads: float32 [16, 2048, 3, 384], P('expert', 'dp')
The draws below stay inside these ranges and needn't reach their ends.
Inputs may be any that keep to these rules, and one draw needn't show every extreme that they name: `expert_ids`: each row names 8 different experts. `held_before`: each expert once. `swap_flags`: entry 0 is always 1; the others are 0 or 1.
All inputs are finite; a program needn't handle non-finite values.
Results may differ from the reference program's by a relative error of at most 0.013.
Values may be sent and summed in bfloat16 or wider, within the bound.
A program may use at most 64 MiB of HBM per device.

```python
import jax
import jax.numpy as jnp
from jax import lax

D = 2048
FF = 384
TOP = 8
TOK_DEV = 64
EXPERTS = 16
CAP = 32
REPLICAS = 16
TOKENS = 16384


def draw_swap_flags(key, part):
    flags = jax.random.randint(jax.random.fold_in(key, 71), (EXPERTS // 2,), 0, 2).astype(jnp.int32)
    return flags.at[0].set(1)


def levels(stream_key, shape, cuts, least, largest):
    loudness = 1.0
    for axis_at, shards_of in cuts:
        draws = jax.random.uniform(jax.random.fold_in(jax.random.fold_in(stream_key, 6), axis_at), (shards_of,), jnp.float32, least / len(cuts), largest / len(cuts))
        loudness = loudness * jnp.repeat(jnp.exp(draws), shape[axis_at] // shards_of).reshape((-1,) + (1,) * (len(shape) - 1 - axis_at))
    return loudness


def picks_of(own_key, rows, number_of, top, lift):
    order = jax.random.permutation(jax.random.fold_in(own_key, 1), number_of)
    pull = order
    for power in range(3):
        pull = pull * pull // number_of
    pull = pull * lift // number_of
    chance = jax.random.randint(jax.random.fold_in(own_key, 2), (rows, number_of), 0, 4096) + pull
    fixed_rows = jax.random.permutation(jax.random.fold_in(own_key, 3), rows)[jnp.arange(number_of) % rows]
    chance = jnp.where(jnp.arange(rows)[:, None] == fixed_rows[None, :], 1 << 14, chance)
    merit = chance * number_of + jnp.arange(number_of)
    return lax.top_k(merit.astype(jnp.int32), top)[1].astype(jnp.int32)


def centred(rng, extent, spread, bound, pieces=(), held_as=jnp.bfloat16):
    values = jax.random.normal(rng, extent, jnp.float32) * spread
    if len(pieces) > 0:
        values = levels(rng, extent, pieces, -0.22, 0.18) * values
    return jnp.clip(values, min=-bound, max=bound).astype(held_as)


def setup_inputs(seed: int = 0) -> dict:
    keys = jax.random.split(jax.random.key(seed), 8)
    return {
        "tokens": centred(keys[0], (TOKENS, D), 1.0, 6.0, ((0, 256),)),
        "cotangent": centred(keys[1], (TOKENS, D), 1.0, 6.0, ((0, 256),)),
        "expert_ids": picks_of(keys[2], TOKENS, EXPERTS, TOP, 8192),
        "gate_probs": jnp.clip(0.05 + 0.45 * jax.random.uniform(keys[3], (TOKENS, TOP), jnp.float32) ** levels(keys[3], (TOKENS, TOP), ((0, 256),), -0.2, 0.2), 0.05, 0.5),
        "held_before": jax.random.permutation(keys[4], EXPERTS).astype(jnp.int32),
        "swap_flags": draw_swap_flags(jax.random.fold_in(keys[7], 71), 0),
        "weights": centred(keys[6], (EXPERTS, D, 3, FF), D ** -0.5, 0.125, ((0, 16),)),
    }


def silu_terms(gate):
    sigma = jax.nn.sigmoid(gate)
    return gate * sigma, sigma * (1.0 + gate * (1.0 - sigma))


def replica_sum(left, right):
    product = jnp.einsum("prd,prf->pdf", left.reshape(REPLICAS, -1, D).astype(jnp.float32), right.reshape(REPLICAS, -1, FF).astype(jnp.float32))
    product = lax.optimization_barrier(product.astype(jnp.bfloat16))
    return jnp.sum(product.astype(jnp.float32), axis=0)


def reference(tokens, cotangent, expert_ids, gate_probs, held_before, swap_flags, weights):
    total_rows = (TOKENS // TOK_DEV) * CAP
    labels = jnp.arange(EXPERTS, dtype=jnp.int32)
    onehot = (expert_ids[:, :, None] == labels[None, None, :]).astype(jnp.int32)
    per_token = jnp.sum(onehot, axis=1).reshape(-1, TOK_DEV, EXPERTS)
    earlier = (jnp.cumsum(per_token, axis=1) - per_token).reshape(TOKENS, EXPERTS)
    rank = jnp.sum(onehot * earlier[:, None, :], axis=2)
    group = jnp.arange(TOKENS, dtype=jnp.int32) // TOK_DEV
    slot_of = jnp.sum((held_before[None, :] == labels[:, None]).astype(jnp.int32) * labels[None, :], axis=1)
    flags_all = jnp.concatenate([swap_flags, swap_flags])
    held_after = jnp.where(flags_all == 1, jnp.roll(held_before, EXPERTS // 2), held_before)
    cot_wide = cotangent.astype(jnp.float32)

    def per_expert(carry, expert):
        mixed_sum, grad_sum, gate_sum = carry
        named = (expert_ids == expert) & (rank < CAP)
        present = jnp.any(named, axis=1)
        rank_here = jnp.sum(jnp.where(named, rank, 0), axis=1).astype(jnp.int32)
        prob_here = jnp.sum(jnp.where(named, gate_probs, jnp.float32(0.0)), axis=1)
        row_index = jnp.where(present, group * CAP + rank_here, total_rows).astype(jnp.int32)
        inputs = jnp.zeros((total_rows, D), jnp.bfloat16).at[row_index].set(tokens, mode="drop")
        matrices = lax.dynamic_index_in_dim(weights, slot_of[expert], 0, keepdims=False)
        w_in = matrices[:, :2, :].reshape(D, 2 * FF)
        w_out = matrices[:, 2, :]
        gate_up = jnp.dot(inputs, w_in, preferred_element_type=jnp.float32)
        gate = gate_up[:, :FF]
        up_part = gate_up[:, FF:]
        silu_value, slope = silu_terms(gate)
        hidden = (silu_value * up_part).astype(jnp.bfloat16)
        outputs = lax.dot_general(hidden, w_out, (((1,), (1,)), ((), ())), preferred_element_type=jnp.float32).astype(jnp.bfloat16)
        picked = outputs.at[row_index].get(mode="fill", fill_value=0).astype(jnp.float32)
        mixed_sum = mixed_sum + prob_here[:, None] * picked
        inner = jnp.sum(cot_wide * picked, axis=1)
        gate_sum = gate_sum + jnp.where(named, inner[:, None], jnp.float32(0.0))
        weighted = (prob_here[:, None] * cot_wide).astype(jnp.bfloat16)
        upstream = jnp.zeros((total_rows, D), jnp.bfloat16).at[row_index].set(weighted, mode="drop")
        d_hidden = jnp.dot(upstream, w_out, preferred_element_type=jnp.float32)
        d_gate = (d_hidden * up_part * slope).astype(jnp.bfloat16)
        d_up = (d_hidden * silu_value).astype(jnp.bfloat16)
        back = lax.dot_general(jnp.concatenate([d_gate, d_up], axis=1), w_in, (((1,), (1,)), ((), ())), preferred_element_type=jnp.float32).astype(jnp.bfloat16)
        grad_sum = grad_sum + back.at[row_index].get(mode="fill", fill_value=0).astype(jnp.float32)
        grads = jnp.stack([replica_sum(inputs, d_gate), replica_sum(inputs, d_up), replica_sum(upstream, hidden)], axis=1)
        return (mixed_sum, grad_sum, gate_sum), grads

    start = (jnp.zeros((TOKENS, D), jnp.float32), jnp.zeros((TOKENS, D), jnp.float32), jnp.zeros((TOKENS, TOP), jnp.float32))
    (mixed_sum, grad_sum, gate_sum), grads = lax.scan(per_expert, start, labels)
    weight_grads = jnp.take(grads, held_after, axis=0)
    return mixed_sum.astype(jnp.bfloat16), grad_sum.astype(jnp.bfloat16), gate_sum, weight_grads
```

```python
import jax
import jax.numpy as jnp
from jax import lax
from jax.experimental import pallas as pl
from jax.experimental.pallas import tpu as pltpu
from jax.sharding import Mesh
from jax.sharding import PartitionSpec as P

DP = ("dp_0", "dp_1")
DP_EXPERT = ("dp_0", "dp_1", "expert")
MESH = pl.DeviceIdType.MESH
F32, BF16 = jnp.float32, jnp.bfloat16
D, FF, CAP = 2048, 384, 32
TOK, HALF = 64, 32
W3 = 3 * FF
GROUPS = ((0,), (1, 2), (3, 4), (5, 6), (7,))
OFFSETS = (0, -1, 1, -2, 2, -3, 3, 4)
SLOT = {o: s for s, o in enumerate(OFFSETS)}
SLOT[-4] = 7


def row(slot, core, half=0):
    return slot * 128 + core * 64 + half * 32


def kernel(
    hb, flags, ids, probs, tok, cot, w,
    mixed_o, tg_o, gg_o, wg_o,
    xall, call, w_in, w_d, up_slope, silu, hidden, whid, dgu, part_m, part_t, acc_m, acc_t,
    ring_m, ring_t, wg, r1, r2, red, q1, q2, share, relay, arrived,
    wsend, wrecv, wcol, ggsend, ggrecv, kept_ids,
    send_sem, recv_sem, local_sem,
):
    px, py, e = lax.axis_index("dp_0"), lax.axis_index("dp_1"), lax.axis_index("expert")
    pz, pc = lax.div(e, 2), lax.rem(e, 2)

    def index_of(off, other):
        return lax.rem(pz + (off + 8), 8) * 2 + (1 - pc if other else pc)

    def along_z(off, other=0):
        return {"expert": index_of(off, other)}

    def along(axis, step):
        return {axis: lax.rem(lax.axis_index(axis) + (step + 4), 4)}

    copies = {}

    def send(key, src, dst, dev):
        n = len(copies)
        copy = pltpu.make_async_remote_copy(
            src_ref=src, dst_ref=dst, send_sem=send_sem.at[n], recv_sem=recv_sem.at[n],
            device_id=dev, device_id_type=MESH,
        )
        copy.start()
        copies[key] = copy

    def arrive(key):
        copies[key].wait_recv()

    barrier = pltpu.get_barrier_semaphore()
    peers = [along_z(o, r) for o in OFFSETS for r in (0, 1) if (o, r) != (0, 0)]
    peers += [along(a, s) for a in DP for s in (1, -1)]
    for peer in peers:
        pl.semaphore_signal(barrier, inc=1, device_id=peer, device_id_type=MESH)

    local = [
        pltpu.make_async_copy(tok, xall.at[pl.ds(0, TOK)], local_sem.at[0]),
        pltpu.make_async_copy(w.at[0], w_in.at[:, pl.ds(0, FF)], local_sem.at[1]),
        pltpu.make_async_copy(w.at[1], w_in.at[:, pl.ds(FF, FF)], local_sem.at[2]),
        pltpu.make_async_copy(w.at[2], w_d, local_sem.at[3]),
        pltpu.make_async_copy(cot, call.at[pl.ds(0, TOK)], local_sem.at[4]),
    ]
    for copy in local:
        copy.start()
    pl.semaphore_wait(barrier, len(peers))

    def gather_own(name, src, dst):
        for d, h in (("L", 0), ("R", 1), ("L", 1), ("R", 0)):
            step = 1 if d == "L" else -1
            send((name, d, 1, h), src.at[pl.ds(32 * h, 32)],
                 dst.at[pl.ds(row(SLOT[-step], 0, h), 32)], along_z(step))
        send((name, "sib", 0), src, dst.at[pl.ds(64, 64)], along_z(0, 1))

    def gather_step(name, dst, s):
        pieces = [("L", 0), ("R", 1)] + ([("L", 1), ("R", 0)] if s < 4 else [])
        for d, h in pieces:
            step = 1 if d == "L" else -1
            slot = SLOT[-step * s]
            here = dst.at[pl.ds(row(slot, 0, h), 32)]
            arrive((name, d, s, h))
            if s < 3 or (s == 3 and (d, h) in (("L", 0), ("R", 1))):
                there = dst.at[pl.ds(row(SLOT[-step * (s + 1)], 0, h), 32)]
                send((name, d, s + 1, h), here, there, along_z(step))
            send((name, "sib", slot, h), here, dst.at[pl.ds(row(slot, 1, h), 32)], along_z(0, 1))

    def gather_sib(name, slots):
        for slot in slots:
            if slot == 0:
                arrive((name, "sib", 0))
            else:
                for h in (0, 1):
                    arrive((name, "sib", slot, h))

    gather_own("x", tok, xall)

    ids8, p8 = ids[...], probs[...]
    ids2 = jnp.concatenate([ids8, ids8], axis=1)
    p2 = jnp.concatenate([p8, p8], axis=1)
    chosen, prob = [], []
    for s, o in enumerate(OFFSETS):
        for r in (0, 1):
            named = ids2 == hb[index_of(o, r)]
            chosen.append(jnp.sum(jnp.where(named, 1.0, 0.0), axis=0, keepdims=True))
            prob.append(jnp.sum(jnp.where(named, p2, 0.0), axis=0, keepdims=True))
    chosen = jnp.concatenate(chosen, axis=0)
    ri = lax.broadcasted_iota(jnp.int32, (128, 128), 0)
    ci = lax.broadcasted_iota(jnp.int32, (128, 128), 1)
    before = jnp.where((ri < ci) & ((ri < 64) == (ci < 64)), 1.0, 0.0).astype(BF16)
    earlier = jnp.dot(chosen.astype(BF16), before, preferred_element_type=F32)
    kept = jnp.where(earlier < CAP - 0.5, 1.0, 0.0)
    weight = jnp.concatenate(prob, axis=0) * kept
    live = jnp.zeros((8, 128), F32)
    for s, o in enumerate(OFFSETS):
        for r in (0, 1):
            n = 2 * s + r
            named = ids2 == hb[index_of(o, r)]
            live = live + jnp.where(named, jnp.broadcast_to(kept[n : n + 1], (8, 128)), 0.0)
            tile = jnp.broadcast_to(weight[n : n + 1], (8, 128))
            wsend[n] = tile
            if n == 0:
                wrecv[0] = tile
            else:
                send(("w", SLOT[-o], r), wsend.at[n], wrecv.at[2 * SLOT[-o] + r], along_z(o, r))
    kept_ids[...] = jnp.where(live > 0.5, ids2, -1)

    gather_own("c", cot, call)
    for copy in local:
        copy.wait()
    for s in range(8):
        for r in (0, 1):
            if s or r:
                arrive(("w", s, r))
    eye = ri == ci
    for s in range(8):
        both = jnp.where(ci < 64, jnp.broadcast_to(wrecv[2 * s, 0:1, :], (128, 128)),
                         jnp.broadcast_to(wrecv[2 * s + 1, 0:1, :], (128, 128)))
        column = jnp.sum(jnp.where(eye, both, 0.0), axis=1, keepdims=True)
        wcol[pl.ds(s * 128, 128), :] = jnp.broadcast_to(column, (128, 128))

    nt = (((1,), (1,)), ((), ()))

    def forward(g):
        slots = GROUPS[g]
        gather_sib("x", slots)
        rows = pl.ds(slots[0] * 128, 128 * len(slots))
        gate_up = jnp.dot(xall[rows, :], w_in[...], preferred_element_type=F32)
        gate, up = gate_up[:, :FF], gate_up[:, FF:]
        sigma = jax.nn.sigmoid(gate)
        act = gate * sigma
        hid = act * up
        silu[rows, :] = act
        up_slope[rows, :] = up * (sigma * (1.0 + gate * (1.0 - sigma)))
        hidden[rows, :] = hid
        scale = wcol[rows, :]
        wh = (hid * jnp.concatenate([scale] * 3, axis=1)).astype(BF16)
        whid[rows, :] = wh
        part_m[rows, :] = lax.dot_general(wh, w_d[...], nt, preferred_element_type=F32).astype(BF16)
        for s in slots:
            send(("sm", s), part_m.at[pl.ds(row(s, 1), 64)], acc_m.at[pl.ds(64 * s, 64)], along_z(0, 1))

    def backward(g):
        slots = GROUPS[g]
        gather_sib("c", slots)
        rows = pl.ds(slots[0] * 128, 128 * len(slots))
        pulled = jnp.dot(call[rows, :], w_d[...], preferred_element_type=F32)
        inner = jnp.sum(pulled * hidden[rows, :], axis=1, keepdims=True)
        scale = wcol[rows, :]
        dh = pulled * jnp.concatenate([scale] * 3, axis=1)
        dgate = (dh * up_slope[rows, :]).astype(BF16)
        dup = (dh * silu[rows, :]).astype(BF16)
        grads = jnp.concatenate([dgate, dup], axis=1)
        dgu[rows, :] = grads
        part_t[rows, :] = lax.dot_general(grads, w_in[...], nt, preferred_element_type=F32).astype(BF16)
        for n, s in enumerate(slots):
            send(("st", s), part_t.at[pl.ds(row(s, 1), 64)], acc_t.at[pl.ds(64 * s, 64)], along_z(0, 1))
            col = jnp.broadcast_to(inner[128 * n : 128 * n + 128], (128, 128))
            line = jnp.sum(jnp.where(eye, col, 0.0), axis=0, keepdims=True)
            ggsend[s] = jnp.broadcast_to(line, (8, 128))
            o = OFFSETS[s]
            for r in (0, 1):
                if (s, r) == (0, 0):
                    ggrecv[0] = jnp.broadcast_to(line, (8, 128))
                else:
                    send(("g", SLOT[-o], r), ggsend.at[s], ggrecv.at[2 * SLOT[-o] + r], along_z(o, r))

    def pair_sum(name, part, acc, slots):
        for s in slots:
            arrive((name, s))
            a = pl.ds(64 * s, 64)
            acc[a, :] = (acc[a, :].astype(F32) + part[pl.ds(row(s, 0), 64), :].astype(F32)).astype(BF16)

    def ring_send(name, acc, ring, d, k, h, src):
        step = 1 if d == 0 else -1
        send((name, d, k - 1, h), src, ring.at[d, pl.ds(64 * (k - 1) + 32 * h, 32)], along_z(step))

    def ring_start(name, acc, ring):
        for d, k, h in ((0, 4, 0), (1, 4, 1), (0, 3, 1), (1, 3, 0)):
            slot = SLOT[k if d == 0 else -k]
            ring_send(name, acc, ring, d, k, h, acc.at[pl.ds(64 * slot + 32 * h, 32)])

    def ring_step(name, acc, ring, k):
        pieces = [(0, 0), (1, 1)] + ([(0, 1), (1, 0)] if k < 3 else [])
        for d, h in pieces:
            arrive((name, d, k, h))
            slot = SLOT[k if d == 0 else -k]
            there = pl.ds(64 * k + 32 * h, 32)
            mine = acc[pl.ds(64 * slot + 32 * h, 32), :].astype(F32)
            ring[d, there, :] = (ring[d, there, :].astype(F32) + mine).astype(BF16)
            ring_send(name, acc, ring, d, k, h, ring.at[d, there])

    def ring_end(name, acc, ring, out):
        for d in (0, 1):
            for h in (0, 1):
                arrive((name, d, 0, h))
        z64 = pl.ds(0, 64)
        total = acc[z64, :].astype(F32) + ring[0, z64, :].astype(F32) + ring[1, z64, :].astype(F32)
        out[...] = total.astype(BF16)

    tn = (((0,), (0,)), ((), ()))

    def weight_terms(blocks):
        cols = []
        for i, j in blocks:
            place = lax.rem(px + i, 4) * 4 + lax.rem(py + j, 4)
            cols.append(pl.ds(pl.multiple_of(place * 128, 128), 128))
        left = jnp.concatenate([xall[:, c] for c in cols], axis=1)
        out = lax.dot_general(left, dgu[...], tn, preferred_element_type=F32)
        for n, (i, j) in enumerate(blocks):
            wg[i, j, :, pl.ds(0, 2 * FF)] = out[128 * n : 128 * n + 128].astype(BF16)
        left = jnp.concatenate([call[:, c] for c in cols], axis=1)
        out = lax.dot_general(left, whid[...], tn, preferred_element_type=F32)
        for n, (i, j) in enumerate(blocks):
            wg[i, j, :, pl.ds(2 * FF, FF)] = out[128 * n : 128 * n + 128].astype(BF16)

    def wg_at(part, first, second):
        rows = pl.ds(64 * part, 64)
        if part == 0:
            return wg.at[first, second, rows]
        return wg.at[second, first, rows]

    def plane_far(part, d):
        send(("far", part, d), wg_at(part, 2, pl.ds(2 * d, 2)), r2.at[part, d], along(DP[part], 1 - 2 * d))

    def plane_near(part, d):
        second = 2 - 2 * d
        send(("near", part, d), wg_at(part, 1 + 2 * d, pl.ds(second, 2)),
             r1.at[part, d, pl.ds(second, 2)], along(DP[part], 1 - 2 * d))

    def plane_chain(part, d):
        arrive(("far", part, d))
        for n in (0, 1):
            mine = wg_at(part, 1 + 2 * d, 2 * d + n)[...].astype(F32)
            r2[part, d, n] = (r2[part, d, n].astype(F32) + mine).astype(BF16)
        send(("chain", part, d), r2.at[part, d], r1.at[part, d, pl.ds(2 * d, 2)], along(DP[part], 1 - 2 * d))

    def plane_turn(part):
        for d in (0, 1):
            arrive(("near", part, d))
            arrive(("chain", part, d))
        axis = DP[1 - part]
        for n in (2, 1, 3, 0):
            total = wg_at(part, 0, n)[...].astype(F32) + r1[part, 0, n].astype(F32) + r1[part, 1, n].astype(F32)
            red[part, n] = total.astype(BF16)
            if n == 2:
                for d in (0, 1):
                    send(("far2", part, d), red.at[part, 2, pl.ds(32 * d, 32)], q2.at[part, d], along(axis, 1 - 2 * d))
            elif n:
                d = 0 if n == 1 else 1
                other = pl.ds(32 - 32 * d, 32)
                send(("near2", part, d), red.at[part, n, other], q1.at[part, d, other], along(axis, 1 - 2 * d))

    def plane_chain2(part):
        axis = DP[1 - part]
        for d in (0, 1):
            arrive(("far2", part, d))
            these = pl.ds(32 * d, 32)
            mine = red[part, 1 + 2 * d, these, :].astype(F32)
            q2[part, d] = (q2[part, d].astype(F32) + mine).astype(BF16)
            send(("chain2", part, d), q2.at[part, d], q1.at[part, d, these], along(axis, 1 - 2 * d))

    def plane_end(part):
        for d in (0, 1):
            arrive(("near2", part, d))
            arrive(("chain2", part, d))
        total = red[part, 0].astype(F32) + q1[part, 0].astype(F32) + q1[part, 1].astype(F32)
        rows = pl.ds(64 * part, 64)
        share[rows, :] = total.astype(BF16)
        send(("swap", part), share.at[rows], relay.at[rows], along_z(2 - 4 * part))

    def swap_relay(part):
        arrive(("swap", part))
        rows = pl.ds(64 * part, 64)
        send(("swap2", part), relay.at[rows], arrived.at[rows], along_z(2 - 4 * part))

    def swap_end(part):
        arrive(("swap2", part))
        rows = pl.ds(64 * part, 64)
        moved = jnp.full((64, W3), flags[lax.rem(e, 8)], jnp.int32) == 1
        mine = jnp.where(moved, arrived[rows, :].astype(F32), share[rows, :].astype(F32))
        for i in range(3):
            wg_o[i, rows, :] = mine[:, i * FF : (i + 1) * FF]

    mixed = ("m", acc_m, ring_m)
    tgrad = ("t", acc_t, ring_t)

    gather_step("x", xall, 1)
    forward(0)
    gather_step("c", call, 1)
    gather_step("x", xall, 2)
    forward(1)
    backward(0)
    gather_step("c", call, 2)
    gather_step("x", xall, 3)
    forward(2)
    backward(1)
    pair_sum("sm", part_m, acc_m, (0, 1, 2, 3, 4))
    gather_step("c", call, 3)
    gather_step("x", xall, 4)
    forward(4)
    forward(3)
    pair_sum("sm", part_m, acc_m, (7, 5, 6))
    ring_start(*mixed)
    backward(2)
    pair_sum("st", part_t, acc_t, (0, 1, 2, 3, 4))
    gather_step("c", call, 4)
    backward(3)
    backward(4)
    pair_sum("st", part_t, acc_t, (7, 5, 6))
    ring_start(*tgrad)
    ring_step(*mixed, 3)
    weight_terms(((2, 0), (2, 1), (0, 2), (1, 2)))
    plane_far(0, 0)
    plane_far(1, 0)
    ring_step(*tgrad, 3)
    weight_terms(((2, 2), (2, 3), (3, 2), (1, 3)))
    plane_far(0, 1)
    plane_far(1, 1)
    plane_near(0, 0)
    ring_step(*mixed, 2)
    weight_terms(((1, 0), (1, 1), (3, 0), (3, 1)))
    plane_near(0, 1)
    plane_near(1, 0)
    plane_chain(0, 0)
    ring_step(*tgrad, 2)
    weight_terms(((3, 3), (0, 1), (0, 3), (0, 0)))
    plane_near(1, 1)
    plane_chain(1, 0)
    plane_chain(0, 1)
    plane_chain(1, 1)
    ring_step(*mixed, 1)
    ring_step(*tgrad, 1)
    for s in range(8):
        for r in (0, 1):
            if s or r:
                arrive(("g", s, r))
    grads = jnp.zeros((8, 128), F32)
    lane = lax.broadcasted_iota(jnp.int32, (8, 128), 1)
    held = kept_ids[...]
    for s, o in enumerate(OFFSETS):
        for r in (0, 1):
            tile = ggrecv[2 * s + r]
            if r:
                tile = pltpu.roll(tile, 64, 1)
            grads = grads + jnp.where(held == hb[index_of(o, r)], tile, 0.0)
    gg_o[...] = grads[:, :64]
    plane_turn(0)
    plane_turn(1)
    ring_end(*mixed, mixed_o)
    plane_chain2(0)
    plane_chain2(1)
    plane_end(0)
    plane_end(1)
    ring_end(*tgrad, tg_o)
    swap_relay(0)
    swap_relay(1)
    swap_end(0)
    swap_end(1)
    for copy in copies.values():
        copy.wait_send()


COPIES = 240


def on_device(tokens, cotangent, expert_ids, gate_probs, held_before, swap_flags, weights):
    vmem = pl.BlockSpec(memory_space=pltpu.VMEM)
    smem = pl.BlockSpec(memory_space=pltpu.SMEM)
    anywhere = pl.BlockSpec(memory_space=pl.ANY)
    rows = 16 * TOK
    scratch = [
        pltpu.VMEM((rows, D), BF16),
        pltpu.VMEM((rows, D), BF16),
        pltpu.VMEM((D, 2 * FF), BF16),
        pltpu.VMEM((D, FF), BF16),
        pltpu.VMEM((rows, FF), F32),
        pltpu.VMEM((rows, FF), F32),
        pltpu.VMEM((rows, FF), F32),
        pltpu.VMEM((rows, FF), BF16),
        pltpu.VMEM((rows, 2 * FF), BF16),
        pltpu.VMEM((rows, D), BF16),
        pltpu.VMEM((rows, D), BF16),
        pltpu.VMEM((rows // 2, D), BF16),
        pltpu.VMEM((rows // 2, D), BF16),
        pltpu.VMEM((2, 4 * TOK, D), BF16),
        pltpu.VMEM((2, 4 * TOK, D), BF16),
        pltpu.VMEM((4, 4, 128, W3), BF16),
        pltpu.VMEM((2, 2, 4, 64, W3), BF16),
        pltpu.VMEM((2, 2, 2, 64, W3), BF16),
        pltpu.VMEM((2, 4, 64, W3), BF16),
        pltpu.VMEM((2, 2, 64, W3), BF16),
        pltpu.VMEM((2, 2, 32, W3), BF16),
        pltpu.VMEM((128, W3), BF16),
        pltpu.VMEM((128, W3), BF16),
        pltpu.VMEM((128, W3), BF16),
        pltpu.VMEM((16, 8, 128), F32),
        pltpu.VMEM((16, 8, 128), F32),
        pltpu.VMEM((rows, 128), F32),
        pltpu.VMEM((8, 8, 128), F32),
        pltpu.VMEM((16, 8, 128), F32),
        pltpu.VMEM((8, 128), jnp.int32),
        pltpu.SemaphoreType.DMA((COPIES,)),
        pltpu.SemaphoreType.DMA((COPIES,)),
        pltpu.SemaphoreType.DMA((5,)),
    ]
    mixed, token_grads, gate_grads, share = pl.pallas_call(
        kernel,
        out_shape=(
            jax.ShapeDtypeStruct((TOK, D), BF16),
            jax.ShapeDtypeStruct((TOK, D), BF16),
            jax.ShapeDtypeStruct((8, TOK), F32),
            jax.ShapeDtypeStruct((3, 128, FF), F32),
        ),
        in_specs=[smem, smem, vmem, vmem, anywhere, anywhere, anywhere],
        out_specs=(vmem, vmem, vmem, vmem),
        scratch_shapes=scratch,
        compiler_params=pltpu.CompilerParams(
            collective_id=0, has_side_effects=True, vmem_limit_bytes=62 * 1024 * 1024
        ),
    )(
        held_before,
        swap_flags,
        expert_ids.T,
        gate_probs.T,
        tokens,
        cotangent,
        jnp.transpose(weights[0], (1, 0, 2)),
    )
    return mixed, token_grads, gate_grads.T, jnp.transpose(share, (1, 0, 2))[None]


def solution(mesh):
    torus = Mesh(mesh.devices.reshape(4, 4, mesh.shape["expert"]), ("dp_0", "dp_1", "expert"))
    in_specs = (
        P(DP_EXPERT, None),
        P(DP_EXPERT, None),
        P(DP_EXPERT, None),
        P(DP_EXPERT, None),
        P(),
        P(),
        P("expert", None, None, None),
    )
    out_specs = (
        P(DP_EXPERT, None),
        P(DP_EXPERT, None),
        P(DP_EXPERT, None),
        P("expert", DP, None, None),
    )
    return jax.shard_map(
        on_device, mesh=torus, in_specs=in_specs, out_specs=out_specs, check_vma=False
    )
```

```python
import jax
import jax.numpy as jnp
from jax import lax
from jax.experimental import pallas as pl
from jax.experimental.pallas import tpu as pltpu
from jax.sharding import Mesh
from jax.sharding import PartitionSpec as P

DP = ("dp_0", "dp_1")
DP_EXPERT = ("dp_0", "dp_1", "expert")
MESH = pl.DeviceIdType.MESH
F32, BF16 = jnp.float32, jnp.bfloat16
D, FF, CAP = 2048, 384, 32
TOK, HALF = 64, 32
W3 = 3 * FF
GROUPS = ((0,), (1, 2), (3, 4), (5, 6), (7,))
OFFSETS = (0, -1, 1, -2, 2, -3, 3, 4)
SLOT = {o: s for s, o in enumerate(OFFSETS)}
SLOT[-4] = 7


def row(slot, core, half=0):
    return slot * 128 + core * 64 + half * 32


def kernel(
    hb, flags, ids, probs, tok, cot, w,
    mixed_h, tg_h, gg_h, wg_h,
    xall, call, w_in, w_d, up_slope, silu, hidden, whid, dgu, part_m, part_t, acc_m, acc_t,
    ring_m, ring_t, wg, r1, r2, red, q1, q2, share, relay, arrived,
    wall, wcol, ggsend, ggrecv, kept_ids, mixed_o, tg_o, gg_o, wg_o,
    send_sem, recv_sem, local_sem,
):
    px, py, e = lax.axis_index("dp_0"), lax.axis_index("dp_1"), lax.axis_index("expert")
    pz, pc = lax.div(e, 2), lax.rem(e, 2)

    def index_of(off, other):
        return lax.rem(pz + (off + 8), 8) * 2 + (1 - pc if other else pc)

    def along_z(off, other=0):
        return {"expert": index_of(off, other)}

    def along(axis, step):
        return {axis: lax.rem(lax.axis_index(axis) + (step + 4), 4)}

    copies = {}

    def send(key, src, dst, dev):
        n = len(copies)
        copy = pltpu.make_async_remote_copy(
            src_ref=src, dst_ref=dst, send_sem=send_sem.at[n], recv_sem=recv_sem.at[n],
            device_id=dev, device_id_type=MESH,
        )
        copy.start()
        copies[key] = copy

    def arrive(key):
        copies[key].wait_recv()

    barrier = pltpu.get_barrier_semaphore()
    peers = [along_z(0, 1), along_z(1), along_z(-1)]
    peers += [along(a, s) for a in DP for s in (1, -1)]
    for peer in peers:
        pl.semaphore_signal(barrier, inc=1, device_id=peer, device_id_type=MESH)

    local = [
        pltpu.make_async_copy(tok, xall.at[pl.ds(0, TOK)], local_sem.at[0]),
        pltpu.make_async_copy(w.at[0], w_in.at[:, pl.ds(0, FF)], local_sem.at[1]),
        pltpu.make_async_copy(w.at[1], w_in.at[:, pl.ds(FF, FF)], local_sem.at[2]),
        pltpu.make_async_copy(w.at[2], w_d, local_sem.at[3]),
        pltpu.make_async_copy(cot, call.at[pl.ds(0, TOK)], local_sem.at[4]),
    ]
    for copy in local:
        copy.start()
    pl.semaphore_wait(barrier, len(peers))

    def gather_own(name, src, dst):
        for d, h in (("L", 0), ("R", 1), ("L", 1), ("R", 0)):
            step = 1 if d == "L" else -1
            send((name, d, 1, h), src.at[pl.ds(32 * h, 32)],
                 dst.at[pl.ds(row(SLOT[-step], 0, h), 32)], along_z(step))
        send((name, "sib", 0), src, dst.at[pl.ds(64, 64)], along_z(0, 1))

    def gather_step(name, dst, s):
        pieces = [("L", 0), ("R", 1)] + ([("L", 1), ("R", 0)] if s < 4 else [])
        for d, h in pieces:
            step = 1 if d == "L" else -1
            slot = SLOT[-step * s]
            here = dst.at[pl.ds(row(slot, 0, h), 32)]
            arrive((name, d, s, h))
            if s < 3 or (s == 3 and (d, h) in (("L", 0), ("R", 1))):
                there = dst.at[pl.ds(row(SLOT[-step * (s + 1)], 0, h), 32)]
                send((name, d, s + 1, h), here, there, along_z(step))
            send((name, "sib", slot, h), here, dst.at[pl.ds(row(slot, 1, h), 32)], along_z(0, 1))

    def weights_own():
        send(("w", "L", 1), wall.at[0], wall.at[2 * SLOT[-1]], along_z(1))
        send(("w", "R", 1), wall.at[0], wall.at[2 * SLOT[1]], along_z(-1))
        send(("w", "sib", 0), wall.at[0], wall.at[1], along_z(0, 1))

    def weights_step(s):
        for d, step in (("L", 1), ("R", -1)):
            if (d, s) == ("R", 4):
                continue
            slot = SLOT[-step * s]
            arrive(("w", d, s))
            if s < (4 if d == "L" else 3):
                send(("w", d, s + 1), wall.at[2 * slot], wall.at[2 * SLOT[-step * (s + 1)]], along_z(step))
            send(("w", "sib", slot), wall.at[2 * slot], wall.at[2 * slot + 1], along_z(0, 1))

    def gather_sib(name, slots):
        for slot in slots:
            if slot == 0:
                arrive((name, "sib", 0))
            else:
                for h in (0, 1):
                    arrive((name, "sib", slot, h))

    gather_own("x", tok, xall)

    ids8, p8 = ids[...], probs[...]
    ids2 = jnp.concatenate([ids8, ids8], axis=1)
    p2 = jnp.concatenate([p8, p8], axis=1)
    chosen, prob = [], []
    for j in range(16):
        named = ids2 == hb[j]
        chosen.append(jnp.sum(jnp.where(named, 1.0, 0.0), axis=0, keepdims=True))
        prob.append(jnp.sum(jnp.where(named, p2, 0.0), axis=0, keepdims=True))
    chosen = jnp.concatenate(chosen, axis=0)
    ri = lax.broadcasted_iota(jnp.int32, (128, 128), 0)
    ci = lax.broadcasted_iota(jnp.int32, (128, 128), 1)
    before = jnp.where((ri < ci) & ((ri < 64) == (ci < 64)), 1.0, 0.0).astype(BF16)
    earlier = jnp.dot(chosen.astype(BF16), before, preferred_element_type=F32)
    kept = jnp.where(earlier < CAP - 0.5, 1.0, 0.0)
    wall[0] = jnp.concatenate(prob, axis=0) * kept
    weights_own()
    gather_own("c", cot, call)
    live = jnp.zeros((8, 128), F32)
    for j in range(16):
        live = live + jnp.where(ids2 == hb[j], jnp.broadcast_to(kept[j : j + 1], (8, 128)), 0.0)
    kept_ids[...] = jnp.where(live > 0.5, ids2, -1)
    for copy in local:
        copy.wait()
    eye = ri == ci

    def weight_columns(slots):
        for s in slots:
            arrive(("w", "sib", s))
            first = jnp.broadcast_to(wall[2 * s, pl.ds(e, 1), :], (128, 128))
            second = jnp.broadcast_to(wall[2 * s + 1, pl.ds(e, 1), :], (128, 128))
            both = jnp.where(ci < 64, first, second)
            column = jnp.sum(jnp.where(eye, both, 0.0), axis=1, keepdims=True)
            wcol[pl.ds(s * 128, 128), :] = jnp.broadcast_to(column, (128, 128))

    nt = (((1,), (1,)), ((), ()))

    def forward(g):
        slots = GROUPS[g]
        weight_columns(slots)
        gather_sib("x", slots)
        rows = pl.ds(slots[0] * 128, 128 * len(slots))
        gate_up = jnp.dot(xall[rows, :], w_in[...], preferred_element_type=F32)
        gate, up = gate_up[:, :FF], gate_up[:, FF:]
        sigma = jax.nn.sigmoid(gate)
        act = gate * sigma
        hid = act * up
        silu[rows, :] = act
        up_slope[rows, :] = up * (sigma * (1.0 + gate * (1.0 - sigma)))
        hidden[rows, :] = hid
        scale = wcol[rows, :]
        wh = (hid * jnp.concatenate([scale] * 3, axis=1)).astype(BF16)
        whid[rows, :] = wh
        part_m[rows, :] = lax.dot_general(wh, w_d[...], nt, preferred_element_type=F32).astype(BF16)
        for s in slots:
            send(("sm", s), part_m.at[pl.ds(row(s, 1), 64)], acc_m.at[pl.ds(64 * s, 64)], along_z(0, 1))

    def backward(g):
        slots = GROUPS[g]
        gather_sib("c", slots)
        rows = pl.ds(slots[0] * 128, 128 * len(slots))
        pulled = jnp.dot(call[rows, :], w_d[...], preferred_element_type=F32)
        inner = jnp.sum(pulled * hidden[rows, :], axis=1, keepdims=True)
        scale = wcol[rows, :]
        dh = pulled * jnp.concatenate([scale] * 3, axis=1)
        dgate = (dh * up_slope[rows, :]).astype(BF16)
        dup = (dh * silu[rows, :]).astype(BF16)
        grads = jnp.concatenate([dgate, dup], axis=1)
        dgu[rows, :] = grads
        part_t[rows, :] = lax.dot_general(grads, w_in[...], nt, preferred_element_type=F32).astype(BF16)
        for n, s in enumerate(slots):
            send(("st", s), part_t.at[pl.ds(row(s, 1), 64)], acc_t.at[pl.ds(64 * s, 64)], along_z(0, 1))
            col = jnp.broadcast_to(inner[128 * n : 128 * n + 128], (128, 128))
            line = jnp.sum(jnp.where(eye, col, 0.0), axis=0, keepdims=True)
            ggsend[s] = jnp.broadcast_to(line, (8, 128))
            o = OFFSETS[s]
            for r in (0, 1):
                if (s, r) == (0, 0):
                    ggrecv[0] = jnp.broadcast_to(line, (8, 128))
                else:
                    send(("g", SLOT[-o], r), ggsend.at[s], ggrecv.at[2 * SLOT[-o] + r], along_z(o, r))

    def pair_sum(name, part, acc, slots):
        for s in slots:
            arrive((name, s))
            a = pl.ds(64 * s, 64)
            acc[a, :] = (acc[a, :].astype(F32) + part[pl.ds(row(s, 0), 64), :].astype(F32)).astype(BF16)

    def ring_send(name, acc, ring, d, k, h, src):
        step = 1 if d == 0 else -1
        send((name, d, k - 1, h), src, ring.at[d, pl.ds(64 * (k - 1) + 32 * h, 32)], along_z(step))

    def ring_start(name, acc, ring):
        for d, k, h in ((0, 4, 0), (1, 4, 1), (0, 3, 1), (1, 3, 0)):
            slot = SLOT[k if d == 0 else -k]
            ring_send(name, acc, ring, d, k, h, acc.at[pl.ds(64 * slot + 32 * h, 32)])

    def ring_step(name, acc, ring, k):
        pieces = [(0, 0), (1, 1)] + ([(0, 1), (1, 0)] if k < 3 else [])
        for d, h in pieces:
            arrive((name, d, k, h))
            slot = SLOT[k if d == 0 else -k]
            there = pl.ds(64 * k + 32 * h, 32)
            mine = acc[pl.ds(64 * slot + 32 * h, 32), :].astype(F32)
            ring[d, there, :] = (ring[d, there, :].astype(F32) + mine).astype(BF16)
            ring_send(name, acc, ring, d, k, h, ring.at[d, there])

    def ring_end(name, acc, ring, out):
        for d in (0, 1):
            for h in (0, 1):
                arrive((name, d, 0, h))
        z64 = pl.ds(0, 64)
        total = acc[z64, :].astype(F32) + ring[0, z64, :].astype(F32) + ring[1, z64, :].astype(F32)
        out[...] = total.astype(BF16)

    tn = (((0,), (0,)), ((), ()))

    def weight_terms(blocks, first, count):
        rows = pl.ds(128 * first, 128 * count)
        cols = []
        for i, j in blocks:
            place = lax.rem(px + i, 4) * 4 + lax.rem(py + j, 4)
            cols.append(pl.ds(pl.multiple_of(place * 128, 128), 128))
        for src, grads, at in ((xall, dgu, 0), (call, whid, 2 * FF)):
            left = jnp.concatenate([src[rows, c] for c in cols], axis=1)
            out = lax.dot_general(left, grads[rows, :], tn, preferred_element_type=F32)
            there = pl.ds(at, out.shape[1])
            for n, (i, j) in enumerate(blocks):
                term = out[128 * n : 128 * n + 128]
                if first:
                    term = term + wg[i, j, :, there].astype(F32)
                wg[i, j, :, there] = term.astype(BF16)

    def wg_at(part, first, second):
        rows = pl.ds(64 * part, 64)
        if part == 0:
            return wg.at[first, second, rows]
        return wg.at[second, first, rows]

    def plane_far(part, d):
        send(("far", part, d), wg_at(part, 2, pl.ds(2 * d, 2)), r2.at[part, d], along(DP[part], 1 - 2 * d))

    def plane_near(part, d):
        second = 2 - 2 * d
        send(("near", part, d), wg_at(part, 1 + 2 * d, pl.ds(second, 2)),
             r1.at[part, d, pl.ds(second, 2)], along(DP[part], 1 - 2 * d))

    def plane_chain(part, d):
        arrive(("far", part, d))
        for n in (0, 1):
            mine = wg_at(part, 1 + 2 * d, 2 * d + n)[...].astype(F32)
            r2[part, d, n] = (r2[part, d, n].astype(F32) + mine).astype(BF16)
        send(("chain", part, d), r2.at[part, d], r1.at[part, d, pl.ds(2 * d, 2)], along(DP[part], 1 - 2 * d))

    def plane_turn(part):
        for d in (0, 1):
            arrive(("near", part, d))
            arrive(("chain", part, d))
        axis = DP[1 - part]
        for n in (2, 1, 3, 0):
            total = wg_at(part, 0, n)[...].astype(F32) + r1[part, 0, n].astype(F32) + r1[part, 1, n].astype(F32)
            red[part, n] = total.astype(BF16)
            if n == 2:
                for d in (0, 1):
                    send(("far2", part, d), red.at[part, 2, pl.ds(32 * d, 32)], q2.at[part, d], along(axis, 1 - 2 * d))
            elif n:
                d = 0 if n == 1 else 1
                other = pl.ds(32 - 32 * d, 32)
                send(("near2", part, d), red.at[part, n, other], q1.at[part, d, other], along(axis, 1 - 2 * d))

    def plane_chain2(part):
        axis = DP[1 - part]
        for d in (0, 1):
            arrive(("far2", part, d))
            these = pl.ds(32 * d, 32)
            mine = red[part, 1 + 2 * d, these, :].astype(F32)
            q2[part, d] = (q2[part, d].astype(F32) + mine).astype(BF16)
            send(("chain2", part, d), q2.at[part, d], q1.at[part, d, these], along(axis, 1 - 2 * d))

    def plane_end(part):
        for d in (0, 1):
            arrive(("near2", part, d))
            arrive(("chain2", part, d))
        total = red[part, 0].astype(F32) + q1[part, 0].astype(F32) + q1[part, 1].astype(F32)
        rows = pl.ds(64 * part, 64)
        share[rows, :] = total.astype(BF16)
        send(("swap", part), share.at[rows], relay.at[rows], along_z(2 - 4 * part))

    def swap_relay(part):
        arrive(("swap", part))
        rows = pl.ds(64 * part, 64)
        send(("swap2", part), relay.at[rows], arrived.at[rows], along_z(2 - 4 * part))

    def swap_end(part):
        arrive(("swap2", part))
        rows = pl.ds(64 * part, 64)
        moved = jnp.full((64, W3), flags[lax.rem(e, 8)], jnp.int32) == 1
        mine = jnp.where(moved, arrived[rows, :].astype(F32), share[rows, :].astype(F32))
        for i in range(3):
            wg_o[i, rows, :] = mine[:, i * FF : (i + 1) * FF]

    mixed = ("m", acc_m, ring_m)
    tgrad = ("t", acc_t, ring_t)
    blocks = (
        ((2, 0), (2, 1), (0, 2), (1, 2)),
        ((2, 2), (2, 3), (3, 2), (1, 3)),
        ((1, 0), (1, 1), (3, 0), (3, 1)),
        ((3, 3), (0, 1), (0, 3), (0, 0)),
    )
    outs = []

    def put(src, dst):
        copy = pltpu.make_async_copy(src, dst, local_sem.at[5 + len(outs)])
        copy.start()
        outs.append(copy)

    gather_step("x", xall, 1)
    weights_step(1)
    forward(0)
    gather_step("c", call, 1)
    gather_step("x", xall, 2)
    weights_step(2)
    forward(1)
    backward(0)
    forward(2)
    gather_step("c", call, 2)
    gather_step("x", xall, 3)
    weights_step(3)
    backward(1)
    forward(3)
    backward(2)
    for some in blocks:
        weight_terms(some, 0, 3)
    pair_sum("sm", part_m, acc_m, (0, 1, 2, 3, 4, 5, 6))
    gather_step("c", call, 3)
    gather_step("x", xall, 4)
    weights_step(4)
    pair_sum("st", part_t, acc_t, (0, 1, 2, 3, 4))
    forward(4)
    pair_sum("sm", part_m, acc_m, (7,))
    ring_start(*mixed)
    backward(3)
    for some in blocks:
        weight_terms(some, 3, 4)
    pair_sum("st", part_t, acc_t, (5, 6))
    gather_step("c", call, 4)
    backward(4)
    ring_step(*mixed, 3)
    pair_sum("st", part_t, acc_t, (7,))
    ring_start(*tgrad)
    weight_terms(blocks[0], 7, 1)
    plane_far(0, 0)
    plane_far(1, 0)
    weight_terms(blocks[1], 7, 1)
    plane_far(0, 1)
    plane_far(1, 1)
    plane_near(0, 0)
    weight_terms(blocks[2], 7, 1)
    plane_near(0, 1)
    plane_near(1, 0)
    weight_terms(blocks[3], 7, 1)
    plane_near(1, 1)
    for d in (0, 1):
        for part in (0, 1):
            plane_chain(part, d)
    ring_step(*mixed, 2)
    ring_step(*tgrad, 3)
    for s in range(8):
        for r in (0, 1):
            if s or r:
                arrive(("g", s, r))
    grads = jnp.zeros((8, 128), F32)
    held = kept_ids[...]
    for s, o in enumerate(OFFSETS):
        for r in (0, 1):
            tile = ggrecv[2 * s + r]
            if r:
                tile = pltpu.roll(tile, 64, 1)
            grads = grads + jnp.where(held == hb[index_of(o, r)], tile, 0.0)
    gg_o[...] = grads[:, :64]
    put(gg_o, gg_h)
    ring_step(*mixed, 1)
    ring_step(*tgrad, 2)
    plane_turn(0)
    plane_turn(1)
    plane_chain2(0)
    plane_chain2(1)
    plane_end(0)
    plane_end(1)
    ring_step(*tgrad, 1)
    swap_relay(0)
    swap_relay(1)
    ring_end(*mixed, mixed_o)
    put(mixed_o, mixed_h)
    ring_end(*tgrad, tg_o)
    put(tg_o, tg_h)
    swap_end(0)
    swap_end(1)
    put(wg_o, wg_h)
    for copy in copies.values():
        copy.wait_send()
    for copy in outs:
        copy.wait()


def hand_on(*refs):
    *pairs, sem = refs
    half = len(pairs) // 2
    copies = [pltpu.make_async_copy(a, b, sem.at[n]) for n, (a, b) in enumerate(zip(pairs[:half], pairs[half:]))]
    for copy in copies:
        copy.start()
    for copy in copies:
        copy.wait()


COPIES = 240


def on_device(tokens, cotangent, expert_ids, gate_probs, held_before, swap_flags, weights):
    vmem = pl.BlockSpec(memory_space=pltpu.VMEM)
    smem = pl.BlockSpec(memory_space=pltpu.SMEM)
    anywhere = pl.BlockSpec(memory_space=pl.ANY)
    rows = 16 * TOK
    scratch = [
        pltpu.VMEM((rows, D), BF16),
        pltpu.VMEM((rows, D), BF16),
        pltpu.VMEM((D, 2 * FF), BF16),
        pltpu.VMEM((D, FF), BF16),
        pltpu.VMEM((rows, FF), F32),
        pltpu.VMEM((rows, FF), F32),
        pltpu.VMEM((rows, FF), F32),
        pltpu.VMEM((rows, FF), BF16),
        pltpu.VMEM((rows, 2 * FF), BF16),
        pltpu.VMEM((rows, D), BF16),
        pltpu.VMEM((rows, D), BF16),
        pltpu.VMEM((rows // 2, D), BF16),
        pltpu.VMEM((rows // 2, D), BF16),
        pltpu.VMEM((2, 4 * TOK, D), BF16),
        pltpu.VMEM((2, 4 * TOK, D), BF16),
        pltpu.VMEM((4, 4, 128, W3), BF16),
        pltpu.VMEM((2, 2, 4, 64, W3), BF16),
        pltpu.VMEM((2, 2, 2, 64, W3), BF16),
        pltpu.VMEM((2, 4, 64, W3), BF16),
        pltpu.VMEM((2, 2, 64, W3), BF16),
        pltpu.VMEM((2, 2, 32, W3), BF16),
        pltpu.VMEM((128, W3), BF16),
        pltpu.VMEM((128, W3), BF16),
        pltpu.VMEM((128, W3), BF16),
        pltpu.VMEM((16, 16, 128), F32),
        pltpu.VMEM((rows, 128), F32),
        pltpu.VMEM((8, 8, 128), F32),
        pltpu.VMEM((16, 8, 128), F32),
        pltpu.VMEM((8, 128), jnp.int32),
        pltpu.VMEM((TOK, D), BF16),
        pltpu.VMEM((TOK, D), BF16),
        pltpu.VMEM((8, TOK), F32),
        pltpu.VMEM((3, 128, FF), F32),
        pltpu.SemaphoreType.DMA((COPIES,)),
        pltpu.SemaphoreType.DMA((COPIES,)),
        pltpu.SemaphoreType.DMA((9,)),
    ]
    results = (
        jax.ShapeDtypeStruct((TOK, D), BF16),
        jax.ShapeDtypeStruct((TOK, D), BF16),
        jax.ShapeDtypeStruct((8, TOK), F32),
        jax.ShapeDtypeStruct((3, 128, FF), F32),
    )
    own = pl.pallas_call(
        kernel,
        out_shape=results,
        in_specs=[smem, smem, vmem, vmem, anywhere, anywhere, anywhere],
        out_specs=(anywhere,) * 4,
        scratch_shapes=scratch,
        compiler_params=pltpu.CompilerParams(
            collective_id=0, has_side_effects=True, vmem_limit_bytes=62 * 1024 * 1024
        ),
    )(
        held_before,
        swap_flags,
        expert_ids.T,
        gate_probs.T,
        tokens,
        cotangent,
        jnp.transpose(weights[0], (1, 0, 2)),
    )
    mixed, token_grads, gate_grads, share = pl.pallas_call(
        hand_on,
        out_shape=results,
        in_specs=[anywhere] * 4,
        out_specs=(anywhere,) * 4,
        scratch_shapes=[pltpu.SemaphoreType.DMA((4,))],
    )(*own)
    return mixed, token_grads, gate_grads.T, jnp.transpose(share, (1, 0, 2))[None]


def solution(mesh):
    torus = Mesh(mesh.devices.reshape(4, 4, mesh.shape["expert"]), ("dp_0", "dp_1", "expert"))
    in_specs = (
        P(DP_EXPERT, None),
        P(DP_EXPERT, None),
        P(DP_EXPERT, None),
        P(DP_EXPERT, None),
        P(),
        P(),
        P("expert", None, None, None),
    )
    out_specs = (
        P(DP_EXPERT, None),
        P(DP_EXPERT, None),
        P(DP_EXPERT, None),
        P("expert", DP, None, None),
    )
    return jax.shard_map(
        on_device, mesh=torus, in_specs=in_specs, out_specs=out_specs, check_vma=False
    )
```

```python
import jax
import jax.numpy as jnp
from jax import lax
from jax.experimental import pallas as pl
from jax.experimental.pallas import tpu as pltpu
from jax.sharding import Mesh
from jax.sharding import PartitionSpec as P

DP = ("dp_0", "dp_1")
DP_EXPERT = ("dp_0", "dp_1", "expert")
MESH = pl.DeviceIdType.MESH
F32, BF16 = jnp.float32, jnp.bfloat16
D, FF, CAP = 2048, 384, 32
TOK, HALF = 64, 32
W3 = 3 * FF
GROUPS = ((0,), (1, 2), (3, 4), (5, 6), (7,))
OFFSETS = (0, -1, 1, -2, 2, -3, 3, 4)
SLOT = {o: s for s, o in enumerate(OFFSETS)}
SLOT[-4] = 7


def row(slot, core, half=0):
    return slot * 128 + core * 64 + half * 32


def kernel(
    hb, flags, ids, probs, tok, cot, w,
    mixed_h, tg_h, gg_h, wg_h,
    xall, call, w_in, w_d, up_slope, silu, hidden, whid, dgu, part_m, part_t, acc_m, acc_t,
    ring_m, ring_t, wg, r1, r2, red, q1, q2, share, relay, arrived,
    wall, wcol, ggsend, ggrecv, kept_ids, mixed_o, tg_o, gg_o, wg_o,
    send_sem, recv_sem, local_sem,
):
    px, py, e = lax.axis_index("dp_0"), lax.axis_index("dp_1"), lax.axis_index("expert")
    pz, pc = lax.div(e, 2), lax.rem(e, 2)

    def index_of(off, other):
        return lax.rem(pz + (off + 8), 8) * 2 + (1 - pc if other else pc)

    def along_z(off, other=0):
        return {"expert": index_of(off, other)}

    def along(axis, step):
        return {axis: lax.rem(lax.axis_index(axis) + (step + 4), 4)}

    copies = {}

    def send(key, src, dst, dev):
        n = len(copies)
        copy = pltpu.make_async_remote_copy(
            src_ref=src, dst_ref=dst, send_sem=send_sem.at[n], recv_sem=recv_sem.at[n],
            device_id=dev, device_id_type=MESH,
        )
        copy.start()
        copies[key] = copy

    def arrive(key):
        copies[key].wait_recv()

    barrier = pltpu.get_barrier_semaphore()
    peers = [along_z(0, 1), along_z(1), along_z(-1)]
    peers += [along(a, s) for a in DP for s in (1, -1)]
    for peer in peers:
        pl.semaphore_signal(barrier, inc=1, device_id=peer, device_id_type=MESH)

    local = [
        pltpu.make_async_copy(tok, xall.at[pl.ds(0, TOK)], local_sem.at[0]),
        pltpu.make_async_copy(w.at[0], w_in.at[:, pl.ds(0, FF)], local_sem.at[1]),
        pltpu.make_async_copy(w.at[1], w_in.at[:, pl.ds(FF, FF)], local_sem.at[2]),
        pltpu.make_async_copy(w.at[2], w_d, local_sem.at[3]),
        pltpu.make_async_copy(cot, call.at[pl.ds(0, TOK)], local_sem.at[4]),
    ]
    for copy in local:
        copy.start()
    pl.semaphore_wait(barrier, len(peers))

    long, short = (("L", 0), ("R", 1)), (("L", 1), ("R", 0))

    def gather_own(name, src, dst, pieces):
        for d, h in pieces:
            step = 1 if d == "L" else -1
            send((name, d, 1, h), src.at[pl.ds(32 * h, 32)],
                 dst.at[pl.ds(row(SLOT[-step], 0, h), 32)], along_z(step))

    def gather_pair(name, src, dst):
        send((name, "sib", 0), src, dst.at[pl.ds(64, 64)], along_z(0, 1))

    def gather_step(name, dst, s):
        for d, h in long + short if s < 4 else long:
            step = 1 if d == "L" else -1
            slot = SLOT[-step * s]
            here = dst.at[pl.ds(row(slot, 0, h), 32)]
            arrive((name, d, s, h))
            if s < 3 or (s == 3 and (d, h) in long):
                there = dst.at[pl.ds(row(SLOT[-step * (s + 1)], 0, h), 32)]
                send((name, d, s + 1, h), here, there, along_z(step))
            send((name, "sib", slot, h), here, dst.at[pl.ds(row(slot, 1, h), 32)], along_z(0, 1))

    def weights_own():
        send(("w", "L", 1), wall.at[0], wall.at[2 * SLOT[-1]], along_z(1))
        send(("w", "R", 1), wall.at[0], wall.at[2 * SLOT[1]], along_z(-1))
        send(("w", "sib", 0), wall.at[0], wall.at[1], along_z(0, 1))

    def weights_step(s):
        for d, step in (("L", 1), ("R", -1)):
            if (d, s) == ("R", 4):
                continue
            slot = SLOT[-step * s]
            arrive(("w", d, s))
            if s < (4 if d == "L" else 3):
                send(("w", d, s + 1), wall.at[2 * slot], wall.at[2 * SLOT[-step * (s + 1)]], along_z(step))
            send(("w", "sib", slot), wall.at[2 * slot], wall.at[2 * slot + 1], along_z(0, 1))

    def gather_sib(name, slots):
        for slot in slots:
            if slot == 0:
                arrive((name, "sib", 0))
            else:
                for h in (0, 1):
                    arrive((name, "sib", slot, h))

    gather_own("x", tok, xall, long + short)
    gather_pair("x", tok, xall)

    ids8, p8 = ids[...], probs[...]
    ids2 = jnp.concatenate([ids8, ids8], axis=1)
    p2 = jnp.concatenate([p8, p8], axis=1)
    chosen, prob = [], []
    for j in range(16):
        named = ids2 == hb[j]
        chosen.append(jnp.sum(jnp.where(named, 1.0, 0.0), axis=0, keepdims=True))
        prob.append(jnp.sum(jnp.where(named, p2, 0.0), axis=0, keepdims=True))
    chosen = jnp.concatenate(chosen, axis=0)
    ri = lax.broadcasted_iota(jnp.int32, (128, 128), 0)
    ci = lax.broadcasted_iota(jnp.int32, (128, 128), 1)
    before = jnp.where((ri < ci) & ((ri < 64) == (ci < 64)), 1.0, 0.0).astype(BF16)
    earlier = jnp.dot(chosen.astype(BF16), before, preferred_element_type=F32)
    kept = jnp.where(earlier < CAP - 0.5, 1.0, 0.0)
    wall[0] = jnp.concatenate(prob, axis=0) * kept
    weights_own()
    gather_own("c", cot, call, long)
    live = jnp.zeros((8, 128), F32)
    for j in range(16):
        live = live + jnp.where(ids2 == hb[j], jnp.broadcast_to(kept[j : j + 1], (8, 128)), 0.0)
    kept_ids[...] = jnp.where(live > 0.5, ids2, -1)
    for copy in local:
        copy.wait()
    eye = ri == ci

    def weight_columns(slots):
        for s in slots:
            arrive(("w", "sib", s))
            first = jnp.broadcast_to(wall[2 * s, pl.ds(e, 1), :], (128, 128))
            second = jnp.broadcast_to(wall[2 * s + 1, pl.ds(e, 1), :], (128, 128))
            both = jnp.where(ci < 64, first, second)
            column = jnp.sum(jnp.where(eye, both, 0.0), axis=1, keepdims=True)
            wcol[pl.ds(s * 128, 128), :] = jnp.broadcast_to(column, (128, 128))

    nt = (((1,), (1,)), ((), ()))

    def forward(g):
        slots = GROUPS[g]
        weight_columns(slots)
        gather_sib("x", slots)
        rows = pl.ds(slots[0] * 128, 128 * len(slots))
        gate_up = jnp.dot(xall[rows, :], w_in[...], preferred_element_type=F32)
        gate, up = gate_up[:, :FF], gate_up[:, FF:]
        sigma = jax.nn.sigmoid(gate)
        act = gate * sigma
        hid = act * up
        silu[rows, :] = act
        up_slope[rows, :] = up * (sigma * (1.0 + gate * (1.0 - sigma)))
        hidden[rows, :] = hid
        scale = wcol[rows, :]
        wh = (hid * jnp.concatenate([scale] * 3, axis=1)).astype(BF16)
        whid[rows, :] = wh
        part_m[rows, :] = lax.dot_general(wh, w_d[...], nt, preferred_element_type=F32).astype(BF16)
        for s in slots:
            send(("sm", s), part_m.at[pl.ds(row(s, 1), 64)], acc_m.at[pl.ds(64 * s, 64)], along_z(0, 1))

    def backward(g):
        slots = GROUPS[g]
        gather_sib("c", slots)
        rows = pl.ds(slots[0] * 128, 128 * len(slots))
        pulled = jnp.dot(call[rows, :], w_d[...], preferred_element_type=F32)
        inner = jnp.sum(pulled * hidden[rows, :], axis=1, keepdims=True)
        scale = wcol[rows, :]
        dh = pulled * jnp.concatenate([scale] * 3, axis=1)
        dgate = (dh * up_slope[rows, :]).astype(BF16)
        dup = (dh * silu[rows, :]).astype(BF16)
        grads = jnp.concatenate([dgate, dup], axis=1)
        dgu[rows, :] = grads
        part_t[rows, :] = lax.dot_general(grads, w_in[...], nt, preferred_element_type=F32).astype(BF16)
        for n, s in enumerate(slots):
            send(("st", s), part_t.at[pl.ds(row(s, 1), 64)], acc_t.at[pl.ds(64 * s, 64)], along_z(0, 1))
            col = jnp.broadcast_to(inner[128 * n : 128 * n + 128], (128, 128))
            line = jnp.sum(jnp.where(eye, col, 0.0), axis=0, keepdims=True)
            ggsend[s] = jnp.broadcast_to(line, (8, 128))
            o = OFFSETS[s]
            for r in (0, 1):
                if (s, r) == (0, 0):
                    ggrecv[0] = jnp.broadcast_to(line, (8, 128))
                else:
                    send(("g", SLOT[-o], r), ggsend.at[s], ggrecv.at[2 * SLOT[-o] + r], along_z(o, r))

    def pair_sum(name, part, acc, slots):
        for s in slots:
            arrive((name, s))
            a = pl.ds(64 * s, 64)
            acc[a, :] = (acc[a, :].astype(F32) + part[pl.ds(row(s, 0), 64), :].astype(F32)).astype(BF16)

    def ring_send(name, acc, ring, d, k, h, src):
        step = 1 if d == 0 else -1
        send((name, d, k - 1, h), src, ring.at[d, pl.ds(64 * (k - 1) + 32 * h, 32)], along_z(step))

    def ring_start(name, acc, ring):
        for d, k, h in ((0, 4, 0), (1, 4, 1), (0, 3, 1), (1, 3, 0)):
            slot = SLOT[k if d == 0 else -k]
            ring_send(name, acc, ring, d, k, h, acc.at[pl.ds(64 * slot + 32 * h, 32)])

    def ring_step(name, acc, ring, k):
        pieces = [(0, 0), (1, 1)] + ([(0, 1), (1, 0)] if k < 3 else [])
        for d, h in pieces:
            arrive((name, d, k, h))
            slot = SLOT[k if d == 0 else -k]
            there = pl.ds(64 * k + 32 * h, 32)
            mine = acc[pl.ds(64 * slot + 32 * h, 32), :].astype(F32)
            ring[d, there, :] = (ring[d, there, :].astype(F32) + mine).astype(BF16)
            ring_send(name, acc, ring, d, k, h, ring.at[d, there])

    def ring_end(name, acc, ring, out):
        for d in (0, 1):
            for h in (0, 1):
                arrive((name, d, 0, h))
        z64 = pl.ds(0, 64)
        total = acc[z64, :].astype(F32) + ring[0, z64, :].astype(F32) + ring[1, z64, :].astype(F32)
        out[...] = total.astype(BF16)

    tn = (((0,), (0,)), ((), ()))

    def weight_terms(blocks, first, count):
        rows = pl.ds(128 * first, 128 * count)
        cols = []
        for i, j in blocks:
            place = lax.rem(px + i, 4) * 4 + lax.rem(py + j, 4)
            cols.append(pl.ds(pl.multiple_of(place * 128, 128), 128))
        for src, grads, at in ((xall, dgu, 0), (call, whid, 2 * FF)):
            left = jnp.concatenate([src[rows, c] for c in cols], axis=1)
            out = lax.dot_general(left, grads[rows, :], tn, preferred_element_type=F32)
            there = pl.ds(at, out.shape[1])
            for n, (i, j) in enumerate(blocks):
                term = out[128 * n : 128 * n + 128]
                if first:
                    term = term + wg[i, j, :, there].astype(F32)
                wg[i, j, :, there] = term.astype(BF16)

    def wg_at(part, first, second):
        rows = pl.ds(64 * part, 64)
        if part == 0:
            return wg.at[first, second, rows]
        return wg.at[second, first, rows]

    def plane_far(part, d):
        send(("far", part, d), wg_at(part, 2, pl.ds(2 * d, 2)), r2.at[part, d], along(DP[part], 1 - 2 * d))

    def plane_near(part, d):
        second = 2 - 2 * d
        send(("near", part, d), wg_at(part, 1 + 2 * d, pl.ds(second, 2)),
             r1.at[part, d, pl.ds(second, 2)], along(DP[part], 1 - 2 * d))

    def plane_chain(part, d):
        arrive(("far", part, d))
        for n in (0, 1):
            mine = wg_at(part, 1 + 2 * d, 2 * d + n)[...].astype(F32)
            r2[part, d, n] = (r2[part, d, n].astype(F32) + mine).astype(BF16)
        send(("chain", part, d), r2.at[part, d], r1.at[part, d, pl.ds(2 * d, 2)], along(DP[part], 1 - 2 * d))

    def plane_turn(part):
        for d in (0, 1):
            arrive(("near", part, d))
            arrive(("chain", part, d))
        axis = DP[1 - part]
        for n in (2, 1, 3, 0):
            total = wg_at(part, 0, n)[...].astype(F32) + r1[part, 0, n].astype(F32) + r1[part, 1, n].astype(F32)
            red[part, n] = total.astype(BF16)
            if n == 2:
                for d in (0, 1):
                    send(("far2", part, d), red.at[part, 2, pl.ds(32 * d, 32)], q2.at[part, d], along(axis, 1 - 2 * d))
            elif n:
                d = 0 if n == 1 else 1
                other = pl.ds(32 - 32 * d, 32)
                send(("near2", part, d), red.at[part, n, other], q1.at[part, d, other], along(axis, 1 - 2 * d))

    def plane_chain2(part):
        axis = DP[1 - part]
        for d in (0, 1):
            arrive(("far2", part, d))
            these = pl.ds(32 * d, 32)
            mine = red[part, 1 + 2 * d, these, :].astype(F32)
            q2[part, d] = (q2[part, d].astype(F32) + mine).astype(BF16)
            send(("chain2", part, d), q2.at[part, d], q1.at[part, d, these], along(axis, 1 - 2 * d))

    def plane_end(part):
        for d in (0, 1):
            arrive(("near2", part, d))
            arrive(("chain2", part, d))
        total = red[part, 0].astype(F32) + q1[part, 0].astype(F32) + q1[part, 1].astype(F32)
        rows = pl.ds(64 * part, 64)
        share[rows, :] = total.astype(BF16)
        send(("swap", part), share.at[rows], relay.at[rows], along_z(2 - 4 * part))

    def swap_relay(part):
        arrive(("swap", part))
        rows = pl.ds(64 * part, 64)
        send(("swap2", part), relay.at[rows], arrived.at[rows], along_z(2 - 4 * part))

    def swap_end(part):
        arrive(("swap2", part))
        rows = pl.ds(64 * part, 64)
        moved = jnp.full((64, W3), flags[lax.rem(e, 8)], jnp.int32) == 1
        mine = jnp.where(moved, arrived[rows, :].astype(F32), share[rows, :].astype(F32))
        for i in range(3):
            wg_o[i, rows, :] = mine[:, i * FF : (i + 1) * FF]

    mixed = ("m", acc_m, ring_m)
    tgrad = ("t", acc_t, ring_t)
    blocks = (
        ((2, 0), (2, 1), (0, 2), (1, 2)),
        ((2, 2), (2, 3), (3, 2), (1, 3)),
        ((1, 0), (1, 1), (3, 0), (3, 1)),
        ((3, 3), (0, 1), (0, 3), (0, 0)),
    )
    outs = []

    def put(src, dst):
        copy = pltpu.make_async_copy(src, dst, local_sem.at[5 + len(outs)])
        copy.start()
        outs.append(copy)

    gather_step("x", xall, 1)
    gather_own("c", cot, call, short)
    weights_step(1)
    gather_pair("c", cot, call)
    forward(0)
    forward(1)
    gather_step("x", xall, 2)
    gather_step("c", call, 1)
    weights_step(2)
    backward(0)
    forward(2)
    backward(1)
    for some in blocks:
        weight_terms(some, 0, 3)
    pair_sum("sm", part_m, acc_m, (0, 1, 2, 3, 4))
    gather_step("x", xall, 3)
    gather_step("c", call, 2)
    weights_step(3)
    forward(3)
    backward(2)
    for some in blocks:
        weight_terms(some, 3, 2)
    pair_sum("sm", part_m, acc_m, (5, 6))
    pair_sum("st", part_t, acc_t, (0, 1, 2, 3, 4))
    gather_step("x", xall, 4)
    gather_step("c", call, 3)
    weights_step(4)
    forward(4)
    pair_sum("sm", part_m, acc_m, (7,))
    ring_start(*mixed)
    backward(3)
    gather_step("c", call, 4)
    backward(4)
    ring_step(*mixed, 3)
    pair_sum("st", part_t, acc_t, (5, 6, 7))
    ring_start(*tgrad)
    weight_terms(blocks[0], 5, 3)
    plane_far(0, 0)
    plane_far(1, 0)
    weight_terms(blocks[1], 5, 3)
    plane_far(0, 1)
    plane_far(1, 1)
    plane_near(0, 0)
    weight_terms(blocks[2], 5, 3)
    plane_near(0, 1)
    plane_near(1, 0)
    weight_terms(blocks[3], 5, 3)
    plane_near(1, 1)
    ring_step(*mixed, 2)
    ring_step(*tgrad, 3)
    for d in (0, 1):
        for part in (0, 1):
            plane_chain(part, d)
    for s in range(8):
        for r in (0, 1):
            if s or r:
                arrive(("g", s, r))
    grads = jnp.zeros((8, 128), F32)
    held = kept_ids[...]
    for s, o in enumerate(OFFSETS):
        for r in (0, 1):
            tile = ggrecv[2 * s + r]
            if r:
                tile = pltpu.roll(tile, 64, 1)
            grads = grads + jnp.where(held == hb[index_of(o, r)], tile, 0.0)
    gg_o[...] = grads[:, :64]
    put(gg_o, gg_h)
    ring_step(*mixed, 1)
    ring_step(*tgrad, 2)
    plane_turn(0)
    plane_turn(1)
    plane_chain2(0)
    plane_chain2(1)
    plane_end(0)
    plane_end(1)
    ring_step(*tgrad, 1)
    swap_relay(0)
    swap_relay(1)
    ring_end(*mixed, mixed_o)
    put(mixed_o, mixed_h)
    ring_end(*tgrad, tg_o)
    put(tg_o, tg_h)
    swap_end(0)
    swap_end(1)
    put(wg_o, wg_h)
    for copy in copies.values():
        copy.wait_send()
    for copy in outs:
        copy.wait()


def hand_on(*refs):
    for src, dst in zip(refs[:4], refs[4:]):
        dst[...] = src[...]


COPIES = 240


def on_device(tokens, cotangent, expert_ids, gate_probs, held_before, swap_flags, weights):
    vmem = pl.BlockSpec(memory_space=pltpu.VMEM)
    smem = pl.BlockSpec(memory_space=pltpu.SMEM)
    anywhere = pl.BlockSpec(memory_space=pl.ANY)
    rows = 16 * TOK
    scratch = [
        pltpu.VMEM((rows, D), BF16),
        pltpu.VMEM((rows, D), BF16),
        pltpu.VMEM((D, 2 * FF), BF16),
        pltpu.VMEM((D, FF), BF16),
        pltpu.VMEM((rows, FF), F32),
        pltpu.VMEM((rows, FF), F32),
        pltpu.VMEM((rows, FF), F32),
        pltpu.VMEM((rows, FF), BF16),
        pltpu.VMEM((rows, 2 * FF), BF16),
        pltpu.VMEM((rows, D), BF16),
        pltpu.VMEM((rows, D), BF16),
        pltpu.VMEM((rows // 2, D), BF16),
        pltpu.VMEM((rows // 2, D), BF16),
        pltpu.VMEM((2, 4 * TOK, D), BF16),
        pltpu.VMEM((2, 4 * TOK, D), BF16),
        pltpu.VMEM((4, 4, 128, W3), BF16),
        pltpu.VMEM((2, 2, 4, 64, W3), BF16),
        pltpu.VMEM((2, 2, 2, 64, W3), BF16),
        pltpu.VMEM((2, 4, 64, W3), BF16),
        pltpu.VMEM((2, 2, 64, W3), BF16),
        pltpu.VMEM((2, 2, 32, W3), BF16),
        pltpu.VMEM((128, W3), BF16),
        pltpu.VMEM((128, W3), BF16),
        pltpu.VMEM((128, W3), BF16),
        pltpu.VMEM((16, 16, 128), F32),
        pltpu.VMEM((rows, 128), F32),
        pltpu.VMEM((8, 8, 128), F32),
        pltpu.VMEM((16, 8, 128), F32),
        pltpu.VMEM((8, 128), jnp.int32),
        pltpu.VMEM((TOK, D), BF16),
        pltpu.VMEM((TOK, D), BF16),
        pltpu.VMEM((8, TOK), F32),
        pltpu.VMEM((3, 128, FF), F32),
        pltpu.SemaphoreType.DMA((COPIES,)),
        pltpu.SemaphoreType.DMA((COPIES,)),
        pltpu.SemaphoreType.DMA((9,)),
    ]
    results = (
        jax.ShapeDtypeStruct((TOK, D), BF16),
        jax.ShapeDtypeStruct((TOK, D), BF16),
        jax.ShapeDtypeStruct((8, TOK), F32),
        jax.ShapeDtypeStruct((3, 128, FF), F32),
    )
    own = pl.pallas_call(
        kernel,
        out_shape=results,
        in_specs=[smem, smem, vmem, vmem, anywhere, anywhere, anywhere],
        out_specs=(anywhere,) * 4,
        scratch_shapes=scratch,
        compiler_params=pltpu.CompilerParams(
            collective_id=0, has_side_effects=True, vmem_limit_bytes=62 * 1024 * 1024
        ),
    )(
        held_before,
        swap_flags,
        expert_ids.T,
        gate_probs.T,
        tokens,
        cotangent,
        jnp.transpose(weights[0], (1, 0, 2)),
    )
    mixed, token_grads, gate_grads, share = pl.pallas_call(
        hand_on,
        out_shape=results,
        in_specs=[vmem] * 4,
        out_specs=(vmem,) * 4,
    )(*own)
    return mixed, token_grads, gate_grads.T, jnp.transpose(share, (1, 0, 2))[None]


def solution(mesh):
    torus = Mesh(mesh.devices.reshape(4, 4, mesh.shape["expert"]), ("dp_0", "dp_1", "expert"))
    in_specs = (
        P(DP_EXPERT, None),
        P(DP_EXPERT, None),
        P(DP_EXPERT, None),
        P(DP_EXPERT, None),
        P(),
        P(),
        P("expert", None, None, None),
    )
    out_specs = (
        P(DP_EXPERT, None),
        P(DP_EXPERT, None),
        P(DP_EXPERT, None),
        P("expert", DP, None, None),
    )
    return jax.shard_map(
        on_device, mesh=torus, in_specs=in_specs, out_specs=out_specs, check_vma=False
    )
```

```python
import jax
import jax.numpy as jnp
from jax import lax
from jax.experimental import pallas as pl
from jax.experimental.pallas import tpu as pltpu
from jax.sharding import Mesh
from jax.sharding import PartitionSpec as P

DP = ("dp_0", "dp_1")
DP_EXPERT = ("dp_0", "dp_1", "expert")
MESH = pl.DeviceIdType.MESH
F32, BF16 = jnp.float32, jnp.bfloat16
D, FF, CAP = 2048, 384, 32
TOK, HALF = 64, 32
W3 = 3 * FF
GROUPS = ((0,), (1, 2), (3, 4), (5, 6), (7,))
OFFSETS = (0, -1, 1, -2, 2, -3, 3, 4)
SLOT = {o: s for s, o in enumerate(OFFSETS)}
SLOT[-4] = 7


def row(slot, core, half=0):
    return slot * 128 + core * 64 + half * 32


def kernel(
    hb, flags, ids, probs, tok, cot, w,
    mixed_o, tg_o, gg_o, wg_o,
    xall, call, w_in, w_d, up_slope, silu, hidden, whid, dgu, part_m, part_t, acc_m, acc_t,
    ring_m, ring_t, wg, r1, r2, red, q1, q2, share, relay, arrived,
    wall, wcol, ggsend, ggrecv, kept_ids,
    send_sem, recv_sem, local_sem,
):
    px, py, e = lax.axis_index("dp_0"), lax.axis_index("dp_1"), lax.axis_index("expert")
    pz, pc = lax.div(e, 2), lax.rem(e, 2)

    def index_of(off, other):
        return lax.rem(pz + (off + 8), 8) * 2 + (1 - pc if other else pc)

    def along_z(off, other=0):
        return {"expert": index_of(off, other)}

    def along(axis, step):
        return {axis: lax.rem(lax.axis_index(axis) + (step + 4), 4)}

    copies = {}

    def send(key, src, dst, dev):
        n = len(copies)
        copy = pltpu.make_async_remote_copy(
            src_ref=src, dst_ref=dst, send_sem=send_sem.at[n], recv_sem=recv_sem.at[n],
            device_id=dev, device_id_type=MESH,
        )
        copy.start()
        copies[key] = copy

    def arrive(key):
        copies[key].wait_recv()

    barrier = pltpu.get_barrier_semaphore()
    peers = [along_z(0, 1), along_z(1), along_z(-1)]
    peers += [along(a, s) for a in DP for s in (1, -1)]
    for peer in peers:
        pl.semaphore_signal(barrier, inc=1, device_id=peer, device_id_type=MESH)

    local = [
        pltpu.make_async_copy(tok, xall.at[pl.ds(0, TOK)], local_sem.at[0]),
        pltpu.make_async_copy(w.at[0], w_in.at[:, pl.ds(0, FF)], local_sem.at[1]),
        pltpu.make_async_copy(w.at[1], w_in.at[:, pl.ds(FF, FF)], local_sem.at[2]),
        pltpu.make_async_copy(w.at[2], w_d, local_sem.at[3]),
        pltpu.make_async_copy(cot, call.at[pl.ds(0, TOK)], local_sem.at[4]),
    ]
    for copy in local:
        copy.start()
    pl.semaphore_wait(barrier, len(peers))

    long, short = (("L", 0), ("R", 1)), (("L", 1), ("R", 0))

    def gather_own(name, src, dst, pieces):
        for d, h in pieces:
            step = 1 if d == "L" else -1
            send((name, d, 1, h), src.at[pl.ds(32 * h, 32)],
                 dst.at[pl.ds(row(SLOT[-step], 0, h), 32)], along_z(step))

    def gather_pair(name, src, dst):
        send((name, "sib", 0), src, dst.at[pl.ds(64, 64)], along_z(0, 1))

    def gather_step(name, dst, s, pieces):
        for d, h in pieces:
            step = 1 if d == "L" else -1
            slot = SLOT[-step * s]
            here = dst.at[pl.ds(row(slot, 0, h), 32)]
            arrive((name, d, s, h))
            if s < 3 or (s == 3 and (d, h) in long):
                there = dst.at[pl.ds(row(SLOT[-step * (s + 1)], 0, h), 32)]
                send((name, d, s + 1, h), here, there, along_z(step))
            send((name, "sib", slot, h), here, dst.at[pl.ds(row(slot, 1, h), 32)], along_z(0, 1))

    def weights_own():
        send(("w", "L", 1), wall.at[0], wall.at[2 * SLOT[-1]], along_z(1))
        send(("w", "R", 1), wall.at[0], wall.at[2 * SLOT[1]], along_z(-1))
        send(("w", "sib", 0), wall.at[0], wall.at[1], along_z(0, 1))

    def weights_step(s):
        for d, step in (("L", 1), ("R", -1)):
            if (d, s) == ("R", 4):
                continue
            slot = SLOT[-step * s]
            arrive(("w", d, s))
            if s < (4 if d == "L" else 3):
                send(("w", d, s + 1), wall.at[2 * slot], wall.at[2 * SLOT[-step * (s + 1)]], along_z(step))
            send(("w", "sib", slot), wall.at[2 * slot], wall.at[2 * slot + 1], along_z(0, 1))

    def gather_sib(name, slots):
        for slot in slots:
            if slot == 0:
                arrive((name, "sib", 0))
            else:
                for h in (0, 1):
                    arrive((name, "sib", slot, h))

    gather_own("x", tok, xall, long + short)
    gather_pair("x", tok, xall)

    ids8, p8 = ids[...], probs[...]
    ids2 = jnp.concatenate([ids8, ids8], axis=1)
    p2 = jnp.concatenate([p8, p8], axis=1)
    chosen, prob = [], []
    for j in range(16):
        named = ids2 == hb[j]
        chosen.append(jnp.sum(jnp.where(named, 1.0, 0.0), axis=0, keepdims=True))
        prob.append(jnp.sum(jnp.where(named, p2, 0.0), axis=0, keepdims=True))
    chosen = jnp.concatenate(chosen, axis=0)
    ri = lax.broadcasted_iota(jnp.int32, (128, 128), 0)
    ci = lax.broadcasted_iota(jnp.int32, (128, 128), 1)
    before = jnp.where((ri < ci) & ((ri < 64) == (ci < 64)), 1.0, 0.0).astype(BF16)
    earlier = jnp.dot(chosen.astype(BF16), before, preferred_element_type=F32)
    kept = jnp.where(earlier < CAP - 0.5, 1.0, 0.0)
    wall[0] = jnp.concatenate(prob, axis=0) * kept
    weights_own()
    gather_own("c", cot, call, long)
    live = jnp.zeros((8, 128), F32)
    for j in range(16):
        live = live + jnp.where(ids2 == hb[j], jnp.broadcast_to(kept[j : j + 1], (8, 128)), 0.0)
    kept_ids[...] = jnp.where(live > 0.5, ids2, -1)
    for copy in local:
        copy.wait()
    eye = ri == ci

    def weight_columns(slots):
        for s in slots:
            arrive(("w", "sib", s))
            first = jnp.broadcast_to(wall[2 * s, pl.ds(e, 1), :], (128, 128))
            second = jnp.broadcast_to(wall[2 * s + 1, pl.ds(e, 1), :], (128, 128))
            both = jnp.where(ci < 64, first, second)
            column = jnp.sum(jnp.where(eye, both, 0.0), axis=1, keepdims=True)
            wcol[pl.ds(s * 128, 128), :] = jnp.broadcast_to(column, (128, 128))

    nt = (((1,), (1,)), ((), ()))

    def forward(g):
        slots = GROUPS[g]
        weight_columns(slots)
        gather_sib("x", slots)
        rows = pl.ds(slots[0] * 128, 128 * len(slots))
        gate_up = jnp.dot(xall[rows, :], w_in[...], preferred_element_type=F32)
        gate, up = gate_up[:, :FF], gate_up[:, FF:]
        sigma = jax.nn.sigmoid(gate)
        act = gate * sigma
        hid = act * up
        silu[rows, :] = act
        up_slope[rows, :] = up * (sigma * (1.0 + gate * (1.0 - sigma)))
        hidden[rows, :] = hid
        scale = wcol[rows, :]
        wh = (hid * jnp.concatenate([scale] * 3, axis=1)).astype(BF16)
        whid[rows, :] = wh
        part_m[rows, :] = lax.dot_general(wh, w_d[...], nt, preferred_element_type=F32).astype(BF16)
        for s in slots:
            send(("sm", s), part_m.at[pl.ds(row(s, 1), 64)], acc_m.at[pl.ds(64 * s, 64)], along_z(0, 1))

    def backward(g):
        slots = GROUPS[g]
        gather_sib("c", slots)
        rows = pl.ds(slots[0] * 128, 128 * len(slots))
        pulled = jnp.dot(call[rows, :], w_d[...], preferred_element_type=F32)
        inner = jnp.sum(pulled * hidden[rows, :], axis=1, keepdims=True)
        scale = wcol[rows, :]
        dh = pulled * jnp.concatenate([scale] * 3, axis=1)
        dgate = (dh * up_slope[rows, :]).astype(BF16)
        dup = (dh * silu[rows, :]).astype(BF16)
        grads = jnp.concatenate([dgate, dup], axis=1)
        dgu[rows, :] = grads
        part_t[rows, :] = lax.dot_general(grads, w_in[...], nt, preferred_element_type=F32).astype(BF16)
        for n, s in enumerate(slots):
            send(("st", s), part_t.at[pl.ds(row(s, 1), 64)], acc_t.at[pl.ds(64 * s, 64)], along_z(0, 1))
            col = jnp.broadcast_to(inner[128 * n : 128 * n + 128], (128, 128))
            line = jnp.sum(jnp.where(eye, col, 0.0), axis=0, keepdims=True)
            ggsend[s] = jnp.broadcast_to(line, (8, 128))
            o = OFFSETS[s]
            for r in (0, 1):
                if (s, r) == (0, 0):
                    ggrecv[0] = jnp.broadcast_to(line, (8, 128))
                else:
                    send(("g", SLOT[-o], r), ggsend.at[s], ggrecv.at[2 * SLOT[-o] + r], along_z(o, r))

    def pair_sum(name, part, acc, slots):
        for s in slots:
            arrive((name, s))
            a = pl.ds(64 * s, 64)
            acc[a, :] = (acc[a, :].astype(F32) + part[pl.ds(row(s, 0), 64), :].astype(F32)).astype(BF16)

    def ring_send(name, acc, ring, d, k, h, src):
        step = 1 if d == 0 else -1
        send((name, d, k - 1, h), src, ring.at[d, pl.ds(64 * (k - 1) + 32 * h, 32)], along_z(step))

    def ring_start(name, acc, ring):
        for d, k, h in ((0, 4, 0), (1, 4, 1), (0, 3, 1), (1, 3, 0)):
            slot = SLOT[k if d == 0 else -k]
            ring_send(name, acc, ring, d, k, h, acc.at[pl.ds(64 * slot + 32 * h, 32)])

    def ring_step(name, acc, ring, k, pieces):
        for way, h in pieces:
            d = 0 if way == "L" else 1
            arrive((name, d, k, h))
            slot = SLOT[k if d == 0 else -k]
            there = pl.ds(64 * k + 32 * h, 32)
            mine = acc[pl.ds(64 * slot + 32 * h, 32), :].astype(F32)
            ring[d, there, :] = (ring[d, there, :].astype(F32) + mine).astype(BF16)
            ring_send(name, acc, ring, d, k, h, ring.at[d, there])

    def ring_end(name, acc, ring, out):
        for d in (0, 1):
            for h in (0, 1):
                arrive((name, d, 0, h))
        z64 = pl.ds(0, 64)
        total = acc[z64, :].astype(F32) + ring[0, z64, :].astype(F32) + ring[1, z64, :].astype(F32)
        out[...] = total.astype(BF16)

    tn = (((0,), (0,)), ((), ()))

    def weight_terms(blocks, first, count):
        rows = pl.ds(128 * first, 128 * count)
        cols = []
        for i, j in blocks:
            place = lax.rem(px + i, 4) * 4 + lax.rem(py + j, 4)
            cols.append(pl.ds(pl.multiple_of(place * 128, 128), 128))
        for src, grads, at in ((xall, dgu, 0), (call, whid, 2 * FF)):
            left = jnp.concatenate([src[rows, c] for c in cols], axis=1)
            out = lax.dot_general(left, grads[rows, :], tn, preferred_element_type=F32)
            there = pl.ds(at, out.shape[1])
            for n, (i, j) in enumerate(blocks):
                term = out[128 * n : 128 * n + 128]
                if first:
                    term = term + wg[i, j, :, there].astype(F32)
                wg[i, j, :, there] = term.astype(BF16)

    def wg_at(part, first, second):
        rows = pl.ds(64 * part, 64)
        if part == 0:
            return wg.at[first, second, rows]
        return wg.at[second, first, rows]

    def plane_far(part, d):
        send(("far", part, d), wg_at(part, 2, pl.ds(2 * d, 2)), r2.at[part, d], along(DP[part], 1 - 2 * d))

    def plane_near(part, d):
        second = 2 - 2 * d
        send(("near", part, d), wg_at(part, 1 + 2 * d, pl.ds(second, 2)),
             r1.at[part, d, pl.ds(second, 2)], along(DP[part], 1 - 2 * d))

    def plane_chain(part, d):
        arrive(("far", part, d))
        for n in (0, 1):
            mine = wg_at(part, 1 + 2 * d, 2 * d + n)[...].astype(F32)
            r2[part, d, n] = (r2[part, d, n].astype(F32) + mine).astype(BF16)
        send(("chain", part, d), r2.at[part, d], r1.at[part, d, pl.ds(2 * d, 2)], along(DP[part], 1 - 2 * d))

    def plane_turn(part):
        for d in (0, 1):
            arrive(("near", part, d))
            arrive(("chain", part, d))
        axis = DP[1 - part]
        for n in (2, 1, 3, 0):
            total = wg_at(part, 0, n)[...].astype(F32) + r1[part, 0, n].astype(F32) + r1[part, 1, n].astype(F32)
            red[part, n] = total.astype(BF16)
            if n == 2:
                for d in (0, 1):
                    send(("far2", part, d), red.at[part, 2, pl.ds(32 * d, 32)], q2.at[part, d], along(axis, 1 - 2 * d))
            elif n:
                d = 0 if n == 1 else 1
                other = pl.ds(32 - 32 * d, 32)
                send(("near2", part, d), red.at[part, n, other], q1.at[part, d, other], along(axis, 1 - 2 * d))

    def plane_chain2(part):
        axis = DP[1 - part]
        for d in (0, 1):
            arrive(("far2", part, d))
            these = pl.ds(32 * d, 32)
            mine = red[part, 1 + 2 * d, these, :].astype(F32)
            q2[part, d] = (q2[part, d].astype(F32) + mine).astype(BF16)
            send(("chain2", part, d), q2.at[part, d], q1.at[part, d, these], along(axis, 1 - 2 * d))

    def plane_end(part):
        for d in (0, 1):
            arrive(("near2", part, d))
            arrive(("chain2", part, d))
        total = red[part, 0].astype(F32) + q1[part, 0].astype(F32) + q1[part, 1].astype(F32)
        rows = pl.ds(64 * part, 64)
        share[rows, :] = total.astype(BF16)
        send(("swap", part), share.at[rows], relay.at[rows], along_z(2 - 4 * part))

    def swap_relay(part):
        arrive(("swap", part))
        rows = pl.ds(64 * part, 64)
        send(("swap2", part), relay.at[rows], arrived.at[rows], along_z(2 - 4 * part))

    def swap_end(part):
        arrive(("swap2", part))
        rows = pl.ds(64 * part, 64)
        moved = jnp.full((64, W3), flags[lax.rem(e, 8)], jnp.int32) == 1
        mine = jnp.where(moved, arrived[rows, :].astype(F32), share[rows, :].astype(F32))
        for i in range(3):
            wg_o[i, rows, :] = mine[:, i * FF : (i + 1) * FF]

    mixed = ("m", acc_m, ring_m)
    tgrad = ("t", acc_t, ring_t)
    blocks = (
        ((2, 0), (2, 1), (0, 2), (1, 2)),
        ((2, 2), (2, 3), (3, 2), (1, 3)),
        ((1, 0), (1, 1), (3, 0), (3, 1)),
        ((3, 3), (0, 1), (0, 3), (0, 0)),
    )
    gather_step("x", xall, 1, long + short)
    gather_own("c", cot, call, short)
    weights_step(1)
    gather_pair("c", cot, call)
    forward(0)
    forward(1)
    gather_step("x", xall, 2, long + short)
    gather_step("c", call, 1, long + short)
    weights_step(2)
    backward(0)
    forward(2)
    backward(1)
    for some in blocks:
        weight_terms(some, 0, 3)
    pair_sum("sm", part_m, acc_m, (0, 1, 2, 3, 4))
    gather_step("x", xall, 3, long + short)
    gather_step("c", call, 2, long + short)
    weights_step(3)
    forward(3)
    backward(2)
    for some in blocks:
        weight_terms(some, 3, 2)
    pair_sum("sm", part_m, acc_m, (5, 6))
    pair_sum("st", part_t, acc_t, (0, 1, 2, 3, 4))
    gather_step("x", xall, 4, long)
    gather_step("c", call, 3, long + short)
    weights_step(4)
    forward(4)
    pair_sum("sm", part_m, acc_m, (7,))
    ring_start(*mixed)
    backward(3)
    gather_step("c", call, 4, long)
    backward(4)
    ring_step(*mixed, 3, long)
    weight_terms(blocks[0], 5, 3)
    plane_far(0, 0)
    plane_far(1, 0)
    weight_terms(blocks[1], 5, 3)
    plane_far(0, 1)
    plane_far(1, 1)
    plane_near(0, 0)
    pair_sum("st", part_t, acc_t, (5, 6, 7))
    ring_start(*tgrad)
    weight_terms(blocks[2], 5, 3)
    plane_near(0, 1)
    plane_near(1, 0)
    weight_terms(blocks[3], 5, 3)
    plane_near(1, 1)
    ring_step(*mixed, 2, long + short)
    for d in (0, 1):
        for part in (0, 1):
            plane_chain(part, d)
    ring_step(*tgrad, 3, long)
    ring_step(*mixed, 1, long + short)
    ring_step(*tgrad, 2, long + short)
    plane_turn(0)
    plane_turn(1)
    plane_chain2(0)
    plane_chain2(1)
    plane_end(0)
    plane_end(1)
    ring_step(*tgrad, 1, long + short)
    swap_relay(0)
    swap_relay(1)
    for s in range(8):
        for r in (0, 1):
            if s or r:
                arrive(("g", s, r))
    grads = jnp.zeros((8, 128), F32)
    held = kept_ids[...]
    for s, o in enumerate(OFFSETS):
        for r in (0, 1):
            tile = ggrecv[2 * s + r]
            if r:
                tile = pltpu.roll(tile, 64, 1)
            grads = grads + jnp.where(held == hb[index_of(o, r)], tile, 0.0)
    gg_o[...] = grads[:, :64]
    ring_end(*mixed, mixed_o)
    ring_end(*tgrad, tg_o)
    swap_end(0)
    swap_end(1)
    for copy in copies.values():
        copy.wait_send()


def hand_on(*refs):
    *refs, sem = refs
    copies = [pltpu.make_async_copy(refs[n], refs[4 + n], sem.at[n]) for n in range(4)]
    for copy in copies:
        copy.start()
    for copy in copies:
        copy.wait()


COPIES = 240


def on_device(tokens, cotangent, expert_ids, gate_probs, held_before, swap_flags, weights):
    vmem = pl.BlockSpec(memory_space=pltpu.VMEM)
    smem = pl.BlockSpec(memory_space=pltpu.SMEM)
    anywhere = pl.BlockSpec(memory_space=pl.ANY)
    rows = 16 * TOK
    scratch = [
        pltpu.VMEM((rows, D), BF16),
        pltpu.VMEM((rows, D), BF16),
        pltpu.VMEM((D, 2 * FF), BF16),
        pltpu.VMEM((D, FF), BF16),
        pltpu.VMEM((rows, FF), F32),
        pltpu.VMEM((rows, FF), F32),
        pltpu.VMEM((rows, FF), F32),
        pltpu.VMEM((rows, FF), BF16),
        pltpu.VMEM((rows, 2 * FF), BF16),
        pltpu.VMEM((rows, D), BF16),
        pltpu.VMEM((rows, D), BF16),
        pltpu.VMEM((rows // 2, D), BF16),
        pltpu.VMEM((rows // 2, D), BF16),
        pltpu.VMEM((2, 4 * TOK, D), BF16),
        pltpu.VMEM((2, 4 * TOK, D), BF16),
        pltpu.VMEM((4, 4, 128, W3), BF16),
        pltpu.VMEM((2, 2, 4, 64, W3), BF16),
        pltpu.VMEM((2, 2, 2, 64, W3), BF16),
        pltpu.VMEM((2, 4, 64, W3), BF16),
        pltpu.VMEM((2, 2, 64, W3), BF16),
        pltpu.VMEM((2, 2, 32, W3), BF16),
        pltpu.VMEM((128, W3), BF16),
        pltpu.VMEM((128, W3), BF16),
        pltpu.VMEM((128, W3), BF16),
        pltpu.VMEM((16, 16, 128), F32),
        pltpu.VMEM((rows, 128), F32),
        pltpu.VMEM((8, 8, 128), F32),
        pltpu.VMEM((16, 8, 128), F32),
        pltpu.VMEM((8, 128), jnp.int32),
        pltpu.SemaphoreType.DMA((COPIES,)),
        pltpu.SemaphoreType.DMA((COPIES,)),
        pltpu.SemaphoreType.DMA((5,)),
    ]
    results = (
        jax.ShapeDtypeStruct((TOK, D), BF16),
        jax.ShapeDtypeStruct((TOK, D), BF16),
        jax.ShapeDtypeStruct((8, TOK), F32),
        jax.ShapeDtypeStruct((3, 128, FF), F32),
    )
    own = pl.pallas_call(
        kernel,
        out_shape=tuple(pltpu.VMEM(r.shape, r.dtype) for r in results),
        in_specs=[smem, smem, vmem, vmem, anywhere, anywhere, anywhere],
        out_specs=(vmem,) * 4,
        scratch_shapes=scratch,
        compiler_params=pltpu.CompilerParams(
            collective_id=0, has_side_effects=True, vmem_limit_bytes=62 * 1024 * 1024
        ),
    )(
        held_before,
        swap_flags,
        expert_ids.T,
        gate_probs.T,
        tokens,
        cotangent,
        jnp.transpose(weights[0], (1, 0, 2)),
    )
    own = [pltpu.with_memory_space_constraint(x, pltpu.VMEM) for x in own]
    mixed, token_grads, gate_grads, share = pl.pallas_call(
        hand_on,
        out_shape=results,
        in_specs=[vmem] * 4,
        out_specs=(anywhere,) * 4,
        scratch_shapes=[pltpu.SemaphoreType.DMA((4,))],
    )(*own)
    return mixed, token_grads, gate_grads.T, jnp.transpose(share, (1, 0, 2))[None]


def solution(mesh):
    torus = Mesh(mesh.devices.reshape(4, 4, mesh.shape["expert"]), ("dp_0", "dp_1", "expert"))
    in_specs = (
        P(DP_EXPERT, None),
        P(DP_EXPERT, None),
        P(DP_EXPERT, None),
        P(DP_EXPERT, None),
        P(),
        P(),
        P("expert", None, None, None),
    )
    out_specs = (
        P(DP_EXPERT, None),
        P(DP_EXPERT, None),
        P(DP_EXPERT, None),
        P("expert", DP, None, None),
    )
    return jax.shard_map(
        on_device, mesh=torus, in_specs=in_specs, out_specs=out_specs, check_vma=False
    )
```

```python
import jax
import jax.numpy as jnp
from jax import lax
from jax.experimental import pallas as pl
from jax.experimental.pallas import tpu as pltpu
from jax.sharding import Mesh
from jax.sharding import PartitionSpec as P

DP = ("dp_0", "dp_1")
DP_EXPERT = ("dp_0", "dp_1", "expert")
MESH = pl.DeviceIdType.MESH
F32, BF16 = jnp.float32, jnp.bfloat16
D, FF, CAP = 2048, 384, 32
TOK, HALF = 64, 32
W3 = 3 * FF
GROUPS = ((0,), (1, 2), (3, 4), (5, 6), (7,))
OFFSETS = (0, -1, 1, -2, 2, -3, 3, 4)
SLOT = {o: s for s, o in enumerate(OFFSETS)}
SLOT[-4] = 7


def row(slot, core, half=0):
    return slot * 128 + core * 64 + half * 32


def kernel(
    hb, flags, ids, probs, tok, cot, w,
    mixed_o, tg_o, gg_o, wg_o,
    xall, call, w_in, w_d, up_slope, silu, hidden, whid, dgu, part_m, part_t, acc_m, acc_t,
    ring_m, ring_t, wg, r1, r2, red, q1, q2, share, relay, arrived,
    wall, wcol, ggsend, ggrecv, kept_ids,
    send_sem, recv_sem, local_sem,
):
    px, py, e = lax.axis_index("dp_0"), lax.axis_index("dp_1"), lax.axis_index("expert")
    pz, pc = lax.div(e, 2), lax.rem(e, 2)

    def index_of(off, other):
        return lax.rem(pz + (off + 8), 8) * 2 + (1 - pc if other else pc)

    def along_z(off, other=0):
        return {"expert": index_of(off, other)}

    def along(axis, step):
        return {axis: lax.rem(lax.axis_index(axis) + (step + 4), 4)}

    copies = {}

    def send(key, src, dst, dev):
        n = len(copies)
        copy = pltpu.make_async_remote_copy(
            src_ref=src, dst_ref=dst, send_sem=send_sem.at[n], recv_sem=recv_sem.at[n],
            device_id=dev, device_id_type=MESH,
        )
        copy.start()
        copies[key] = copy

    def arrive(key):
        copies[key].wait_recv()

    barrier = pltpu.get_barrier_semaphore()
    peers = [along_z(0, 1), along_z(1), along_z(-1)]
    peers += [along(a, s) for a in DP for s in (1, -1)]
    for peer in peers:
        pl.semaphore_signal(barrier, inc=1, device_id=peer, device_id_type=MESH)

    local = [
        pltpu.make_async_copy(tok, xall.at[pl.ds(0, TOK)], local_sem.at[0]),
        pltpu.make_async_copy(w.at[0], w_in.at[:, pl.ds(0, FF)], local_sem.at[1]),
        pltpu.make_async_copy(w.at[1], w_in.at[:, pl.ds(FF, FF)], local_sem.at[2]),
        pltpu.make_async_copy(w.at[2], w_d, local_sem.at[3]),
        pltpu.make_async_copy(cot, call.at[pl.ds(0, TOK)], local_sem.at[4]),
    ]
    for copy in local:
        copy.start()
    pl.semaphore_wait(barrier, len(peers))

    long, short = (("L", 0), ("R", 1)), (("L", 1), ("R", 0))

    def gather_own(name, src, dst, pieces):
        for d, h in pieces:
            step = 1 if d == "L" else -1
            send((name, d, 1, h), src.at[pl.ds(32 * h, 32)],
                 dst.at[pl.ds(row(SLOT[-step], 0, h), 32)], along_z(step))

    def gather_pair(name, src, dst):
        send((name, "sib", 0), src, dst.at[pl.ds(64, 64)], along_z(0, 1))

    def gather_step(name, dst, s, pieces):
        for d, h in pieces:
            step = 1 if d == "L" else -1
            slot = SLOT[-step * s]
            here = dst.at[pl.ds(row(slot, 0, h), 32)]
            arrive((name, d, s, h))
            if s < 3 or (s == 3 and (d, h) in long):
                there = dst.at[pl.ds(row(SLOT[-step * (s + 1)], 0, h), 32)]
                send((name, d, s + 1, h), here, there, along_z(step))
            send((name, "sib", slot, h), here, dst.at[pl.ds(row(slot, 1, h), 32)], along_z(0, 1))

    def weights_own():
        send(("w", "L", 1), wall.at[0], wall.at[2 * SLOT[-1]], along_z(1))
        send(("w", "R", 1), wall.at[0], wall.at[2 * SLOT[1]], along_z(-1))
        send(("w", "sib", 0), wall.at[0], wall.at[1], along_z(0, 1))

    def weights_step(s):
        for d, step in (("L", 1), ("R", -1)):
            if (d, s) == ("R", 4):
                continue
            slot = SLOT[-step * s]
            arrive(("w", d, s))
            if s < (4 if d == "L" else 3):
                send(("w", d, s + 1), wall.at[2 * slot], wall.at[2 * SLOT[-step * (s + 1)]], along_z(step))
            send(("w", "sib", slot), wall.at[2 * slot], wall.at[2 * slot + 1], along_z(0, 1))

    def gather_sib(name, slots):
        for slot in slots:
            if slot == 0:
                arrive((name, "sib", 0))
            else:
                for h in (0, 1):
                    arrive((name, "sib", slot, h))

    gather_own("x", tok, xall, long + short)
    gather_pair("x", tok, xall)

    ids8, p8 = ids[...], probs[...]
    ids2 = jnp.concatenate([ids8, ids8], axis=1)
    p2 = jnp.concatenate([p8, p8], axis=1)
    chosen, prob = [], []
    for j in range(16):
        named = ids2 == hb[j]
        chosen.append(jnp.sum(jnp.where(named, 1.0, 0.0), axis=0, keepdims=True))
        prob.append(jnp.sum(jnp.where(named, p2, 0.0), axis=0, keepdims=True))
    chosen = jnp.concatenate(chosen, axis=0)
    ri = lax.broadcasted_iota(jnp.int32, (128, 128), 0)
    ci = lax.broadcasted_iota(jnp.int32, (128, 128), 1)
    before = jnp.where((ri < ci) & ((ri < 64) == (ci < 64)), 1.0, 0.0).astype(BF16)
    earlier = jnp.dot(chosen.astype(BF16), before, preferred_element_type=F32)
    kept = jnp.where(earlier < CAP - 0.5, 1.0, 0.0)
    wall[0] = jnp.concatenate(prob, axis=0) * kept
    weights_own()
    gather_own("c", cot, call, long)
    live = jnp.zeros((8, 128), F32)
    for j in range(16):
        live = live + jnp.where(ids2 == hb[j], jnp.broadcast_to(kept[j : j + 1], (8, 128)), 0.0)
    kept_ids[...] = jnp.where(live > 0.5, ids2, -1)
    for copy in local:
        copy.wait()
    eye = ri == ci

    def weight_columns(slots):
        for s in slots:
            arrive(("w", "sib", s))
            first = jnp.broadcast_to(wall[2 * s, pl.ds(e, 1), :], (128, 128))
            second = jnp.broadcast_to(wall[2 * s + 1, pl.ds(e, 1), :], (128, 128))
            both = jnp.where(ci < 64, first, second)
            column = jnp.sum(jnp.where(eye, both, 0.0), axis=1, keepdims=True)
            wcol[pl.ds(s * 128, 128), :] = jnp.broadcast_to(column, (128, 128))

    nt = (((1,), (1,)), ((), ()))

    def forward(g):
        slots = GROUPS[g]
        weight_columns(slots)
        gather_sib("x", slots)
        rows = pl.ds(slots[0] * 128, 128 * len(slots))
        gate_up = jnp.dot(xall[rows, :], w_in[...], preferred_element_type=F32)
        gate, up = gate_up[:, :FF], gate_up[:, FF:]
        sigma = jax.nn.sigmoid(gate)
        act = gate * sigma
        hid = act * up
        silu[rows, :] = act
        up_slope[rows, :] = up * (sigma * (1.0 + gate * (1.0 - sigma)))
        hidden[rows, :] = hid
        scale = wcol[rows, :]
        wh = (hid * jnp.concatenate([scale] * 3, axis=1)).astype(BF16)
        whid[rows, :] = wh
        part_m[rows, :] = lax.dot_general(wh, w_d[...], nt, preferred_element_type=F32).astype(BF16)
        for s in slots:
            send(("sm", s), part_m.at[pl.ds(row(s, 1), 64)], acc_m.at[pl.ds(64 * s, 64)], along_z(0, 1))

    def backward(g):
        slots = GROUPS[g]
        gather_sib("c", slots)
        rows = pl.ds(slots[0] * 128, 128 * len(slots))
        pulled = jnp.dot(call[rows, :], w_d[...], preferred_element_type=F32)
        inner = jnp.sum(pulled * hidden[rows, :], axis=1, keepdims=True)
        scale = wcol[rows, :]
        dh = pulled * jnp.concatenate([scale] * 3, axis=1)
        dgate = (dh * up_slope[rows, :]).astype(BF16)
        dup = (dh * silu[rows, :]).astype(BF16)
        grads = jnp.concatenate([dgate, dup], axis=1)
        dgu[rows, :] = grads
        part_t[rows, :] = lax.dot_general(grads, w_in[...], nt, preferred_element_type=F32).astype(BF16)
        for n, s in enumerate(slots):
            send(("st", s), part_t.at[pl.ds(row(s, 1), 64)], acc_t.at[pl.ds(64 * s, 64)], along_z(0, 1))
            col = jnp.broadcast_to(inner[128 * n : 128 * n + 128], (128, 128))
            line = jnp.sum(jnp.where(eye, col, 0.0), axis=0, keepdims=True)
            ggsend[s] = jnp.broadcast_to(line, (8, 128))
            o = OFFSETS[s]
            for r in (0, 1):
                if (s, r) == (0, 0):
                    ggrecv[0] = jnp.broadcast_to(line, (8, 128))
                else:
                    send(("g", SLOT[-o], r), ggsend.at[s], ggrecv.at[2 * SLOT[-o] + r], along_z(o, r))

    def pair_sum(name, part, acc, slots):
        for s in slots:
            arrive((name, s))
            a = pl.ds(64 * s, 64)
            acc[a, :] = (acc[a, :].astype(F32) + part[pl.ds(row(s, 0), 64), :].astype(F32)).astype(BF16)

    def ring_send(name, acc, ring, d, k, h, src):
        step = 1 if d == 0 else -1
        send((name, d, k - 1, h), src, ring.at[d, pl.ds(64 * (k - 1) + 32 * h, 32)], along_z(step))

    def ring_start(name, acc, ring, pieces):
        k = 4 if pieces == long else 3
        for way, h in pieces:
            d = 0 if way == "L" else 1
            slot = SLOT[k if d == 0 else -k]
            ring_send(name, acc, ring, d, k, h, acc.at[pl.ds(64 * slot + 32 * h, 32)])

    def ring_step(name, acc, ring, k, pieces):
        for way, h in pieces:
            d = 0 if way == "L" else 1
            arrive((name, d, k, h))
            slot = SLOT[k if d == 0 else -k]
            there = pl.ds(64 * k + 32 * h, 32)
            mine = acc[pl.ds(64 * slot + 32 * h, 32), :].astype(F32)
            ring[d, there, :] = (ring[d, there, :].astype(F32) + mine).astype(BF16)
            ring_send(name, acc, ring, d, k, h, ring.at[d, there])

    def ring_end(name, acc, ring, out):
        for d in (0, 1):
            for h in (0, 1):
                arrive((name, d, 0, h))
        z64 = pl.ds(0, 64)
        total = acc[z64, :].astype(F32) + ring[0, z64, :].astype(F32) + ring[1, z64, :].astype(F32)
        out[...] = total.astype(BF16)

    tn = (((0,), (0,)), ((), ()))

    def weight_terms(blocks, first, count):
        rows = pl.ds(128 * first, 128 * count)
        cols = []
        for i, j in blocks:
            place = lax.rem(px + i, 4) * 4 + lax.rem(py + j, 4)
            cols.append(pl.ds(pl.multiple_of(place * 128, 128), 128))
        for src, grads, at in ((xall, dgu, 0), (call, whid, 2 * FF)):
            left = jnp.concatenate([src[rows, c] for c in cols], axis=1)
            out = lax.dot_general(left, grads[rows, :], tn, preferred_element_type=F32)
            there = pl.ds(at, out.shape[1])
            for n, (i, j) in enumerate(blocks):
                term = out[128 * n : 128 * n + 128]
                if first:
                    term = term + wg[i, j, :, there].astype(F32)
                wg[i, j, :, there] = term.astype(BF16)

    def wg_at(part, first, second):
        rows = pl.ds(64 * part, 64)
        if part == 0:
            return wg.at[first, second, rows]
        return wg.at[second, first, rows]

    def plane_far(part, d):
        send(("far", part, d), wg_at(part, 2, pl.ds(2 * d, 2)), r2.at[part, d], along(DP[part], 1 - 2 * d))

    def plane_near(part, d):
        second = 2 - 2 * d
        send(("near", part, d), wg_at(part, 1 + 2 * d, pl.ds(second, 2)),
             r1.at[part, d, pl.ds(second, 2)], along(DP[part], 1 - 2 * d))

    def plane_chain(part, d):
        arrive(("far", part, d))
        for n in (0, 1):
            mine = wg_at(part, 1 + 2 * d, 2 * d + n)[...].astype(F32)
            r2[part, d, n] = (r2[part, d, n].astype(F32) + mine).astype(BF16)
        send(("chain", part, d), r2.at[part, d], r1.at[part, d, pl.ds(2 * d, 2)], along(DP[part], 1 - 2 * d))

    def plane_turn(part):
        for d in (0, 1):
            arrive(("near", part, d))
            arrive(("chain", part, d))
        axis = DP[1 - part]
        for n in (2, 1, 3, 0):
            total = wg_at(part, 0, n)[...].astype(F32) + r1[part, 0, n].astype(F32) + r1[part, 1, n].astype(F32)
            red[part, n] = total.astype(BF16)
            if n == 2:
                for d in (0, 1):
                    send(("far2", part, d), red.at[part, 2, pl.ds(32 * d, 32)], q2.at[part, d], along(axis, 1 - 2 * d))
            elif n:
                d = 0 if n == 1 else 1
                other = pl.ds(32 - 32 * d, 32)
                send(("near2", part, d), red.at[part, n, other], q1.at[part, d, other], along(axis, 1 - 2 * d))

    def plane_chain2(part):
        axis = DP[1 - part]
        for d in (0, 1):
            arrive(("far2", part, d))
            these = pl.ds(32 * d, 32)
            mine = red[part, 1 + 2 * d, these, :].astype(F32)
            q2[part, d] = (q2[part, d].astype(F32) + mine).astype(BF16)
            send(("chain2", part, d), q2.at[part, d], q1.at[part, d, these], along(axis, 1 - 2 * d))

    def plane_end(part):
        for d in (0, 1):
            arrive(("near2", part, d))
            arrive(("chain2", part, d))
        total = red[part, 0].astype(F32) + q1[part, 0].astype(F32) + q1[part, 1].astype(F32)
        rows = pl.ds(64 * part, 64)
        share[rows, :] = total.astype(BF16)
        send(("swap", part), share.at[rows], relay.at[rows], along_z(2 - 4 * part))

    def swap_relay(part):
        arrive(("swap", part))
        rows = pl.ds(64 * part, 64)
        send(("swap2", part), relay.at[rows], arrived.at[rows], along_z(2 - 4 * part))

    def swap_end(part):
        arrive(("swap2", part))
        rows = pl.ds(64 * part, 64)
        moved = jnp.full((64, W3), flags[lax.rem(e, 8)], jnp.int32) == 1
        mine = jnp.where(moved, arrived[rows, :].astype(F32), share[rows, :].astype(F32))
        for i in range(3):
            wg_o[i, rows, :] = mine[:, i * FF : (i + 1) * FF]

    mixed = ("m", acc_m, ring_m)
    tgrad = ("t", acc_t, ring_t)
    blocks = (
        ((2, 0), (2, 1), (0, 2), (1, 2)),
        ((2, 2), (2, 3), (3, 2), (1, 3)),
        ((1, 0), (1, 1), (3, 0), (3, 1)),
        ((3, 3), (0, 1), (0, 3), (0, 0)),
    )
    gather_step("x", xall, 1, long + short)
    gather_own("c", cot, call, short)
    weights_step(1)
    gather_pair("c", cot, call)
    forward(0)
    forward(1)
    gather_step("x", xall, 2, long + short)
    gather_step("c", call, 1, long + short)
    weights_step(2)
    backward(0)
    forward(2)
    backward(1)
    for some in blocks:
        weight_terms(some, 0, 3)
    pair_sum("sm", part_m, acc_m, (0, 1, 2, 3, 4))
    gather_step("x", xall, 3, long + short)
    gather_step("c", call, 2, long + short)
    weights_step(3)
    forward(3)
    backward(2)
    for some in blocks:
        weight_terms(some, 3, 2)
    pair_sum("sm", part_m, acc_m, (5, 6))
    pair_sum("st", part_t, acc_t, (0, 1, 2, 3, 4))
    gather_step("x", xall, 4, long)
    gather_step("c", call, 3, long + short)
    weights_step(4)
    forward(4)
    ring_start(*mixed, short)
    backward(3)
    pair_sum("sm", part_m, acc_m, (7,))
    ring_start(*mixed, long)
    gather_step("c", call, 4, long)
    backward(4)
    weight_terms(blocks[0], 5, 3)
    plane_far(0, 0)
    plane_far(1, 0)
    weight_terms(blocks[1], 5, 3)
    plane_far(0, 1)
    plane_far(1, 1)
    plane_near(0, 0)
    ring_step(*mixed, 3, long)
    pair_sum("st", part_t, acc_t, (5, 6, 7))
    ring_start(*tgrad, long)
    ring_start(*tgrad, short)
    weight_terms(blocks[2], 5, 3)
    plane_near(0, 1)
    plane_near(1, 0)
    weight_terms(blocks[3], 5, 3)
    plane_near(1, 1)
    ring_step(*mixed, 2, long + short)
    for d in (0, 1):
        for part in (0, 1):
            plane_chain(part, d)
    ring_step(*tgrad, 3, long)
    ring_step(*mixed, 1, long + short)
    ring_step(*tgrad, 2, long + short)
    plane_turn(0)
    plane_turn(1)
    plane_chain2(0)
    plane_chain2(1)
    plane_end(0)
    plane_end(1)
    ring_step(*tgrad, 1, long + short)
    swap_relay(0)
    swap_relay(1)
    for s in range(8):
        for r in (0, 1):
            if s or r:
                arrive(("g", s, r))
    grads = jnp.zeros((8, 128), F32)
    held = kept_ids[...]
    for s, o in enumerate(OFFSETS):
        for r in (0, 1):
            tile = ggrecv[2 * s + r]
            if r:
                tile = pltpu.roll(tile, 64, 1)
            grads = grads + jnp.where(held == hb[index_of(o, r)], tile, 0.0)
    gg_o[...] = grads[:, :64]
    ring_end(*mixed, mixed_o)
    ring_end(*tgrad, tg_o)
    swap_end(0)
    swap_end(1)
    for copy in copies.values():
        copy.wait_send()


def hand_on(*refs):
    *refs, sem = refs
    copies = [pltpu.make_async_copy(refs[n], refs[4 + n], sem.at[n]) for n in range(4)]
    for copy in copies:
        copy.start()
    for copy in copies:
        copy.wait()


COPIES = 240


def on_device(tokens, cotangent, expert_ids, gate_probs, held_before, swap_flags, weights):
    vmem = pl.BlockSpec(memory_space=pltpu.VMEM)
    smem = pl.BlockSpec(memory_space=pltpu.SMEM)
    anywhere = pl.BlockSpec(memory_space=pl.ANY)
    rows = 16 * TOK
    scratch = [
        pltpu.VMEM((rows, D), BF16),
        pltpu.VMEM((rows, D), BF16),
        pltpu.VMEM((D, 2 * FF), BF16),
        pltpu.VMEM((D, FF), BF16),
        pltpu.VMEM((rows, FF), F32),
        pltpu.VMEM((rows, FF), F32),
        pltpu.VMEM((rows, FF), F32),
        pltpu.VMEM((rows, FF), BF16),
        pltpu.VMEM((rows, 2 * FF), BF16),
        pltpu.VMEM((rows, D), BF16),
        pltpu.VMEM((rows, D), BF16),
        pltpu.VMEM((rows // 2, D), BF16),
        pltpu.VMEM((rows // 2, D), BF16),
        pltpu.VMEM((2, 4 * TOK, D), BF16),
        pltpu.VMEM((2, 4 * TOK, D), BF16),
        pltpu.VMEM((4, 4, 128, W3), BF16),
        pltpu.VMEM((2, 2, 4, 64, W3), BF16),
        pltpu.VMEM((2, 2, 2, 64, W3), BF16),
        pltpu.VMEM((2, 4, 64, W3), BF16),
        pltpu.VMEM((2, 2, 64, W3), BF16),
        pltpu.VMEM((2, 2, 32, W3), BF16),
        pltpu.VMEM((128, W3), BF16),
        pltpu.VMEM((128, W3), BF16),
        pltpu.VMEM((128, W3), BF16),
        pltpu.VMEM((16, 16, 128), F32),
        pltpu.VMEM((rows, 128), F32),
        pltpu.VMEM((8, 8, 128), F32),
        pltpu.VMEM((16, 8, 128), F32),
        pltpu.VMEM((8, 128), jnp.int32),
        pltpu.SemaphoreType.DMA((COPIES,)),
        pltpu.SemaphoreType.DMA((COPIES,)),
        pltpu.SemaphoreType.DMA((5,)),
    ]
    results = (
        jax.ShapeDtypeStruct((TOK, D), BF16),
        jax.ShapeDtypeStruct((TOK, D), BF16),
        jax.ShapeDtypeStruct((8, TOK), F32),
        jax.ShapeDtypeStruct((3, 128, FF), F32),
    )
    own = pl.pallas_call(
        kernel,
        out_shape=tuple(pltpu.VMEM(r.shape, r.dtype) for r in results),
        in_specs=[smem, smem, vmem, vmem, anywhere, anywhere, anywhere],
        out_specs=(vmem,) * 4,
        scratch_shapes=scratch,
        compiler_params=pltpu.CompilerParams(
            collective_id=0, has_side_effects=True, vmem_limit_bytes=62 * 1024 * 1024
        ),
    )(
        held_before,
        swap_flags,
        expert_ids.T,
        gate_probs.T,
        tokens,
        cotangent,
        jnp.transpose(weights[0], (1, 0, 2)),
    )
    own = [pltpu.with_memory_space_constraint(x, pltpu.VMEM) for x in own]
    mixed, token_grads, gate_grads, share = pl.pallas_call(
        hand_on,
        out_shape=results,
        in_specs=[vmem] * 4,
        out_specs=(anywhere,) * 4,
        scratch_shapes=[pltpu.SemaphoreType.DMA((4,))],
    )(*own)
    return mixed, token_grads, gate_grads.T, jnp.transpose(share, (1, 0, 2))[None]


def solution(mesh):
    torus = Mesh(mesh.devices.reshape(4, 4, mesh.shape["expert"]), ("dp_0", "dp_1", "expert"))
    in_specs = (
        P(DP_EXPERT, None),
        P(DP_EXPERT, None),
        P(DP_EXPERT, None),
        P(DP_EXPERT, None),
        P(),
        P(),
        P("expert", None, None, None),
    )
    out_specs = (
        P(DP_EXPERT, None),
        P(DP_EXPERT, None),
        P(DP_EXPERT, None),
        P("expert", DP, None, None),
    )
    return jax.shard_map(
        on_device, mesh=torus, in_specs=in_specs, out_specs=out_specs, check_vma=False
    )
```

```python
import jax
import jax.numpy as jnp
from jax import lax
from jax.experimental import pallas as pl
from jax.experimental.pallas import tpu as pltpu
from jax.sharding import Mesh
from jax.sharding import PartitionSpec as P

DP = ("dp_0", "dp_1")
DP_EXPERT = ("dp_0", "dp_1", "expert")
MESH = pl.DeviceIdType.MESH
F32, BF16 = jnp.float32, jnp.bfloat16
D, FF, CAP = 2048, 384, 32
TOK, HALF = 64, 32
W3 = 3 * FF
GROUPS = ((0,), (1, 2), (3, 4), (5, 6), (7,))
OFFSETS = (0, -1, 1, -2, 2, -3, 3, 4)
SLOT = {o: s for s, o in enumerate(OFFSETS)}
SLOT[-4] = 7


def row(slot, core, half=0):
    return slot * 128 + core * 64 + half * 32


def kernel(
    hb, flags, ids, probs, tok, cot, w,
    mixed_o, tg_o, gg_o, wg_o,
    xall, call, w_in, w_d, up_slope, silu, hidden, whid, dgu, part_m, part_t, acc_m, acc_t,
    ring_m, ring_t, wg, r1, r2, red, q1, q2, share, relay, arrived,
    wall, wcol, ggsend, ggrecv, kept_ids,
    send_sem, recv_sem, local_sem,
):
    px, py, e = lax.axis_index("dp_0"), lax.axis_index("dp_1"), lax.axis_index("expert")
    pz, pc = lax.div(e, 2), lax.rem(e, 2)

    def index_of(off, other):
        return lax.rem(pz + (off + 8), 8) * 2 + (1 - pc if other else pc)

    def along_z(off, other=0):
        return {"expert": index_of(off, other)}

    def along(axis, step):
        return {axis: lax.rem(lax.axis_index(axis) + (step + 4), 4)}

    copies = {}

    def send(key, src, dst, dev):
        n = len(copies)
        copy = pltpu.make_async_remote_copy(
            src_ref=src, dst_ref=dst, send_sem=send_sem.at[n], recv_sem=recv_sem.at[n],
            device_id=dev, device_id_type=MESH,
        )
        copy.start()
        copies[key] = copy

    def arrive(key):
        copies[key].wait_recv()

    barrier = pltpu.get_barrier_semaphore()
    peers = [along_z(0, 1), along_z(1), along_z(-1)]
    peers += [along(a, s) for a in DP for s in (1, -1)]
    for peer in peers:
        pl.semaphore_signal(barrier, inc=1, device_id=peer, device_id_type=MESH)

    local = [
        pltpu.make_async_copy(tok, xall.at[pl.ds(0, TOK)], local_sem.at[0]),
        pltpu.make_async_copy(w.at[0], w_in.at[:, pl.ds(0, FF)], local_sem.at[1]),
        pltpu.make_async_copy(w.at[1], w_in.at[:, pl.ds(FF, FF)], local_sem.at[2]),
        pltpu.make_async_copy(w.at[2], w_d, local_sem.at[3]),
        pltpu.make_async_copy(cot, call.at[pl.ds(0, TOK)], local_sem.at[4]),
    ]
    for copy in local:
        copy.start()
    pl.semaphore_wait(barrier, len(peers))

    long, short = (("L", 0), ("R", 1)), (("L", 1), ("R", 0))

    def gather_own(name, src, dst, pieces):
        for d, h in pieces:
            step = 1 if d == "L" else -1
            send((name, d, 1, h), src.at[pl.ds(32 * h, 32)],
                 dst.at[pl.ds(row(SLOT[-step], 0, h), 32)], along_z(step))

    def gather_pair(name, src, dst):
        send((name, "sib", 0), src, dst.at[pl.ds(64, 64)], along_z(0, 1))

    def gather_step(name, dst, s, pieces):
        for d, h in pieces:
            step = 1 if d == "L" else -1
            slot = SLOT[-step * s]
            here = dst.at[pl.ds(row(slot, 0, h), 32)]
            arrive((name, d, s, h))
            if s < 3 or (s == 3 and (d, h) in long):
                there = dst.at[pl.ds(row(SLOT[-step * (s + 1)], 0, h), 32)]
                send((name, d, s + 1, h), here, there, along_z(step))
            send((name, "sib", slot, h), here, dst.at[pl.ds(row(slot, 1, h), 32)], along_z(0, 1))

    def weights_own():
        send(("w", "L", 1), wall.at[0], wall.at[2 * SLOT[-1]], along_z(1))
        send(("w", "R", 1), wall.at[0], wall.at[2 * SLOT[1]], along_z(-1))
        send(("w", "sib", 0), wall.at[0], wall.at[1], along_z(0, 1))

    def weights_step(s):
        for d, step in (("L", 1), ("R", -1)):
            if (d, s) == ("R", 4):
                continue
            slot = SLOT[-step * s]
            arrive(("w", d, s))
            if s < (4 if d == "L" else 3):
                send(("w", d, s + 1), wall.at[2 * slot], wall.at[2 * SLOT[-step * (s + 1)]], along_z(step))
            send(("w", "sib", slot), wall.at[2 * slot], wall.at[2 * slot + 1], along_z(0, 1))

    def gather_sib(name, slots):
        for slot in slots:
            if slot == 0:
                arrive((name, "sib", 0))
            else:
                for h in (0, 1):
                    arrive((name, "sib", slot, h))

    gather_own("x", tok, xall, long + short)
    gather_pair("x", tok, xall)

    ids8, p8 = ids[...], probs[...]
    ids2 = jnp.concatenate([ids8, ids8], axis=1)
    p2 = jnp.concatenate([p8, p8], axis=1)
    chosen, prob = [], []
    for j in range(16):
        named = ids2 == hb[j]
        chosen.append(jnp.sum(jnp.where(named, 1.0, 0.0), axis=0, keepdims=True))
        prob.append(jnp.sum(jnp.where(named, p2, 0.0), axis=0, keepdims=True))
    chosen = jnp.concatenate(chosen, axis=0)
    ri = lax.broadcasted_iota(jnp.int32, (128, 128), 0)
    ci = lax.broadcasted_iota(jnp.int32, (128, 128), 1)
    before = jnp.where((ri < ci) & ((ri < 64) == (ci < 64)), 1.0, 0.0).astype(BF16)
    earlier = jnp.dot(chosen.astype(BF16), before, preferred_element_type=F32)
    kept = jnp.where(earlier < CAP - 0.5, 1.0, 0.0)
    wall[0] = jnp.concatenate(prob, axis=0) * kept
    weights_own()
    gather_own("c", cot, call, long)
    live = jnp.zeros((8, 128), F32)
    for j in range(16):
        live = live + jnp.where(ids2 == hb[j], jnp.broadcast_to(kept[j : j + 1], (8, 128)), 0.0)
    kept_ids[...] = jnp.where(live > 0.5, ids2, -1)
    for copy in local:
        copy.wait()
    eye = ri == ci

    def weight_columns(slots):
        for s in slots:
            arrive(("w", "sib", s))
            first = jnp.broadcast_to(wall[2 * s, pl.ds(e, 1), :], (128, 128))
            second = jnp.broadcast_to(wall[2 * s + 1, pl.ds(e, 1), :], (128, 128))
            both = jnp.where(ci < 64, first, second)
            column = jnp.sum(jnp.where(eye, both, 0.0), axis=1, keepdims=True)
            wcol[pl.ds(s * 128, 128), :] = jnp.broadcast_to(column, (128, 128))

    nt = (((1,), (1,)), ((), ()))

    def forward(g):
        slots = GROUPS[g]
        weight_columns(slots)
        gather_sib("x", slots)
        rows = pl.ds(slots[0] * 128, 128 * len(slots))
        gate_up = jnp.dot(xall[rows, :], w_in[...], preferred_element_type=F32)
        gate, up = gate_up[:, :FF], gate_up[:, FF:]
        sigma = jax.nn.sigmoid(gate)
        act = gate * sigma
        hid = act * up
        silu[rows, :] = act
        up_slope[rows, :] = up * (sigma * (1.0 + gate * (1.0 - sigma)))
        hidden[rows, :] = hid
        scale = wcol[rows, :]
        wh = (hid * jnp.concatenate([scale] * 3, axis=1)).astype(BF16)
        whid[rows, :] = wh
        part_m[rows, :] = lax.dot_general(wh, w_d[...], nt, preferred_element_type=F32).astype(BF16)
        for s in slots:
            send(("sm", s), part_m.at[pl.ds(row(s, 1), 64)], acc_m.at[pl.ds(64 * s, 64)], along_z(0, 1))

    def backward(g):
        slots = GROUPS[g]
        gather_sib("c", slots)
        rows = pl.ds(slots[0] * 128, 128 * len(slots))
        pulled = jnp.dot(call[rows, :], w_d[...], preferred_element_type=F32)
        inner = jnp.sum(pulled * hidden[rows, :], axis=1, keepdims=True)
        scale = wcol[rows, :]
        dh = pulled * jnp.concatenate([scale] * 3, axis=1)
        dgate = (dh * up_slope[rows, :]).astype(BF16)
        dup = (dh * silu[rows, :]).astype(BF16)
        grads = jnp.concatenate([dgate, dup], axis=1)
        dgu[rows, :] = grads
        part_t[rows, :] = lax.dot_general(grads, w_in[...], nt, preferred_element_type=F32).astype(BF16)
        for n, s in enumerate(slots):
            send(("st", s), part_t.at[pl.ds(row(s, 1), 64)], acc_t.at[pl.ds(64 * s, 64)], along_z(0, 1))
            col = jnp.broadcast_to(inner[128 * n : 128 * n + 128], (128, 128))
            line = jnp.sum(jnp.where(eye, col, 0.0), axis=0, keepdims=True)
            ggsend[s] = jnp.broadcast_to(line, (8, 128))
            o = OFFSETS[s]
            for r in (0, 1):
                if (s, r) == (0, 0):
                    ggrecv[0] = jnp.broadcast_to(line, (8, 128))
                else:
                    send(("g", SLOT[-o], r), ggsend.at[s], ggrecv.at[2 * SLOT[-o] + r], along_z(o, r))

    def pair_sum(name, part, acc, slots):
        for s in slots:
            arrive((name, s))
            a = pl.ds(64 * s, 64)
            acc[a, :] = (acc[a, :].astype(F32) + part[pl.ds(row(s, 0), 64), :].astype(F32)).astype(BF16)

    def ring_send(name, acc, ring, d, k, h, src):
        step = 1 if d == 0 else -1
        send((name, d, k - 1, h), src, ring.at[d, pl.ds(64 * (k - 1) + 32 * h, 32)], along_z(step))

    def ring_start(name, acc, ring):
        for d, k, h in ((0, 4, 0), (1, 4, 1), (0, 3, 1), (1, 3, 0)):
            slot = SLOT[k if d == 0 else -k]
            ring_send(name, acc, ring, d, k, h, acc.at[pl.ds(64 * slot + 32 * h, 32)])

    def ring_step(name, acc, ring, k, pieces):
        for way, h in pieces:
            d = 0 if way == "L" else 1
            arrive((name, d, k, h))
            slot = SLOT[k if d == 0 else -k]
            there = pl.ds(64 * k + 32 * h, 32)
            mine = acc[pl.ds(64 * slot + 32 * h, 32), :].astype(F32)
            ring[d, there, :] = (ring[d, there, :].astype(F32) + mine).astype(BF16)
            ring_send(name, acc, ring, d, k, h, ring.at[d, there])

    def ring_end(name, acc, ring, out):
        for d in (0, 1):
            for h in (0, 1):
                arrive((name, d, 0, h))
        z64 = pl.ds(0, 64)
        total = acc[z64, :].astype(F32) + ring[0, z64, :].astype(F32) + ring[1, z64, :].astype(F32)
        out[...] = total.astype(BF16)

    tn = (((0,), (0,)), ((), ()))

    def weight_terms(blocks, first, count):
        rows = pl.ds(128 * first, 128 * count)
        cols = []
        for i, j in blocks:
            place = lax.rem(px + i, 4) * 4 + lax.rem(py + j, 4)
            cols.append(pl.ds(pl.multiple_of(place * 128, 128), 128))
        for src, grads, at in ((xall, dgu, 0), (call, whid, 2 * FF)):
            left = jnp.concatenate([src[rows, c] for c in cols], axis=1)
            out = lax.dot_general(left, grads[rows, :], tn, preferred_element_type=F32)
            there = pl.ds(at, out.shape[1])
            for n, (i, j) in enumerate(blocks):
                term = out[128 * n : 128 * n + 128]
                if first:
                    term = term + wg[i, j, :, there].astype(F32)
                wg[i, j, :, there] = term.astype(BF16)

    def wg_at(part, first, second):
        rows = pl.ds(64 * part, 64)
        if part == 0:
            return wg.at[first, second, rows]
        return wg.at[second, first, rows]

    def plane_far(part, d):
        send(("far", part, d), wg_at(part, 2, pl.ds(2 * d, 2)), r2.at[part, d], along(DP[part], 1 - 2 * d))

    def plane_near(part, d):
        second = 2 - 2 * d
        send(("near", part, d), wg_at(part, 1 + 2 * d, pl.ds(second, 2)),
             r1.at[part, d, pl.ds(second, 2)], along(DP[part], 1 - 2 * d))

    def plane_chain(part, d):
        arrive(("far", part, d))
        for n in (0, 1):
            mine = wg_at(part, 1 + 2 * d, 2 * d + n)[...].astype(F32)
            r2[part, d, n] = (r2[part, d, n].astype(F32) + mine).astype(BF16)
        send(("chain", part, d), r2.at[part, d], r1.at[part, d, pl.ds(2 * d, 2)], along(DP[part], 1 - 2 * d))

    def plane_turn(part):
        for d in (0, 1):
            arrive(("near", part, d))
            arrive(("chain", part, d))
        axis = DP[1 - part]
        for n in (2, 1, 3, 0):
            total = wg_at(part, 0, n)[...].astype(F32) + r1[part, 0, n].astype(F32) + r1[part, 1, n].astype(F32)
            red[part, n] = total.astype(BF16)
            if n == 2:
                for d in (0, 1):
                    send(("far2", part, d), red.at[part, 2, pl.ds(32 * d, 32)], q2.at[part, d], along(axis, 1 - 2 * d))
            elif n:
                d = 0 if n == 1 else 1
                other = pl.ds(32 - 32 * d, 32)
                send(("near2", part, d), red.at[part, n, other], q1.at[part, d, other], along(axis, 1 - 2 * d))

    def plane_chain2(part):
        axis = DP[1 - part]
        for d in (0, 1):
            arrive(("far2", part, d))
            these = pl.ds(32 * d, 32)
            mine = red[part, 1 + 2 * d, these, :].astype(F32)
            q2[part, d] = (q2[part, d].astype(F32) + mine).astype(BF16)
            send(("chain2", part, d), q2.at[part, d], q1.at[part, d, these], along(axis, 1 - 2 * d))

    def plane_end(part):
        for d in (0, 1):
            arrive(("near2", part, d))
            arrive(("chain2", part, d))
        total = red[part, 0].astype(F32) + q1[part, 0].astype(F32) + q1[part, 1].astype(F32)
        rows = pl.ds(64 * part, 64)
        share[rows, :] = total.astype(BF16)
        send(("swap", part), share.at[rows], relay.at[rows], along_z(2 - 4 * part))

    def swap_relay(part):
        arrive(("swap", part))
        rows = pl.ds(64 * part, 64)
        send(("swap2", part), relay.at[rows], arrived.at[rows], along_z(2 - 4 * part))

    def swap_end(part):
        arrive(("swap2", part))
        rows = pl.ds(64 * part, 64)
        moved = jnp.full((64, W3), flags[lax.rem(e, 8)], jnp.int32) == 1
        mine = jnp.where(moved, arrived[rows, :].astype(F32), share[rows, :].astype(F32))
        for i in range(3):
            wg_o[i, rows, :] = mine[:, i * FF : (i + 1) * FF]

    mixed = ("m", acc_m, ring_m)
    tgrad = ("t", acc_t, ring_t)
    blocks = (
        ((2, 0), (2, 1), (0, 2), (1, 2)),
        ((2, 2), (2, 3), (3, 2), (1, 3)),
        ((1, 0), (1, 1), (3, 0), (3, 1)),
        ((3, 3), (0, 1), (0, 3), (0, 0)),
    )
    gather_step("x", xall, 1, long + short)
    gather_own("c", cot, call, short)
    weights_step(1)
    gather_pair("c", cot, call)
    forward(0)
    forward(1)
    gather_step("x", xall, 2, long + short)
    gather_step("c", call, 1, long + short)
    weights_step(2)
    backward(0)
    forward(2)
    backward(1)
    for some in blocks:
        weight_terms(some, 0, 3)
    pair_sum("sm", part_m, acc_m, (0, 1, 2, 3, 4))
    gather_step("x", xall, 3, long + short)
    gather_step("c", call, 2, long + short)
    weights_step(3)
    forward(3)
    backward(2)
    for some in blocks:
        weight_terms(some, 3, 2)
    pair_sum("sm", part_m, acc_m, (5, 6))
    pair_sum("st", part_t, acc_t, (0, 1, 2, 3, 4))
    gather_step("x", xall, 4, long)
    gather_step("c", call, 3, long + short)
    weights_step(4)
    forward(4)
    backward(3)
    pair_sum("sm", part_m, acc_m, (7,))
    ring_start(*mixed)
    gather_step("c", call, 4, long)
    backward(4)
    weight_terms(blocks[0], 5, 3)
    plane_far(0, 0)
    plane_far(1, 0)
    weight_terms(blocks[1], 5, 3)
    plane_far(0, 1)
    plane_far(1, 1)
    plane_near(0, 0)
    ring_step(*mixed, 3, long)
    pair_sum("st", part_t, acc_t, (5, 6, 7))
    ring_start(*tgrad)
    weight_terms(blocks[2], 5, 3)
    plane_near(0, 1)
    plane_near(1, 0)
    weight_terms(blocks[3], 5, 3)
    plane_near(1, 1)
    for d in (0, 1):
        for part in (0, 1):
            plane_chain(part, d)
    ring_step(*mixed, 2, long + short)
    ring_step(*tgrad, 3, long)
    ring_step(*mixed, 1, long + short)
    plane_turn(0)
    plane_turn(1)
    ring_step(*tgrad, 2, long + short)
    plane_chain2(0)
    plane_chain2(1)
    plane_end(0)
    plane_end(1)
    ring_step(*tgrad, 1, long + short)
    swap_relay(0)
    swap_relay(1)
    for s in range(8):
        for r in (0, 1):
            if s or r:
                arrive(("g", s, r))
    grads = jnp.zeros((8, 128), F32)
    held = kept_ids[...]
    for s, o in enumerate(OFFSETS):
        for r in (0, 1):
            tile = ggrecv[2 * s + r]
            if r:
                tile = pltpu.roll(tile, 64, 1)
            grads = grads + jnp.where(held == hb[index_of(o, r)], tile, 0.0)
    gg_o[...] = grads[:, :64]
    ring_end(*mixed, mixed_o)
    ring_end(*tgrad, tg_o)
    swap_end(0)
    swap_end(1)
    for copy in copies.values():
        copy.wait_send()


def hand_on(*refs):
    *refs, sem = refs
    copies = [pltpu.make_async_copy(refs[n], refs[4 + n], sem.at[n]) for n in range(4)]
    for copy in copies:
        copy.start()
    for copy in copies:
        copy.wait()


COPIES = 240


def on_device(tokens, cotangent, expert_ids, gate_probs, held_before, swap_flags, weights):
    vmem = pl.BlockSpec(memory_space=pltpu.VMEM)
    smem = pl.BlockSpec(memory_space=pltpu.SMEM)
    anywhere = pl.BlockSpec(memory_space=pl.ANY)
    rows = 16 * TOK
    scratch = [
        pltpu.VMEM((rows, D), BF16),
        pltpu.VMEM((rows, D), BF16),
        pltpu.VMEM((D, 2 * FF), BF16),
        pltpu.VMEM((D, FF), BF16),
        pltpu.VMEM((rows, FF), F32),
        pltpu.VMEM((rows, FF), F32),
        pltpu.VMEM((rows, FF), F32),
        pltpu.VMEM((rows, FF), BF16),
        pltpu.VMEM((rows, 2 * FF), BF16),
        pltpu.VMEM((rows, D), BF16),
        pltpu.VMEM((rows, D), BF16),
        pltpu.VMEM((rows // 2, D), BF16),
        pltpu.VMEM((rows // 2, D), BF16),
        pltpu.VMEM((2, 4 * TOK, D), BF16),
        pltpu.VMEM((2, 4 * TOK, D), BF16),
        pltpu.VMEM((4, 4, 128, W3), BF16),
        pltpu.VMEM((2, 2, 4, 64, W3), BF16),
        pltpu.VMEM((2, 2, 2, 64, W3), BF16),
        pltpu.VMEM((2, 4, 64, W3), BF16),
        pltpu.VMEM((2, 2, 64, W3), BF16),
        pltpu.VMEM((2, 2, 32, W3), BF16),
        pltpu.VMEM((128, W3), BF16),
        pltpu.VMEM((128, W3), BF16),
        pltpu.VMEM((128, W3), BF16),
        pltpu.VMEM((16, 16, 128), F32),
        pltpu.VMEM((rows, 128), F32),
        pltpu.VMEM((8, 8, 128), F32),
        pltpu.VMEM((16, 8, 128), F32),
        pltpu.VMEM((8, 128), jnp.int32),
        pltpu.SemaphoreType.DMA((COPIES,)),
        pltpu.SemaphoreType.DMA((COPIES,)),
        pltpu.SemaphoreType.DMA((5,)),
    ]
    results = (
        jax.ShapeDtypeStruct((TOK, D), BF16),
        jax.ShapeDtypeStruct((TOK, D), BF16),
        jax.ShapeDtypeStruct((8, TOK), F32),
        jax.ShapeDtypeStruct((3, 128, FF), F32),
    )
    own = pl.pallas_call(
        kernel,
        out_shape=tuple(pltpu.VMEM(r.shape, r.dtype) for r in results),
        in_specs=[smem, smem, vmem, vmem, anywhere, anywhere, anywhere],
        out_specs=(vmem,) * 4,
        scratch_shapes=scratch,
        compiler_params=pltpu.CompilerParams(
            collective_id=0, has_side_effects=True, vmem_limit_bytes=62 * 1024 * 1024
        ),
    )(
        held_before,
        swap_flags,
        expert_ids.T,
        gate_probs.T,
        tokens,
        cotangent,
        jnp.transpose(weights[0], (1, 0, 2)),
    )
    own = [pltpu.with_memory_space_constraint(x, pltpu.VMEM) for x in own]
    mixed, token_grads, gate_grads, share = pl.pallas_call(
        hand_on,
        out_shape=results,
        in_specs=[vmem] * 4,
        out_specs=(anywhere,) * 4,
        scratch_shapes=[pltpu.SemaphoreType.DMA((4,))],
    )(*own)
    return mixed, token_grads, gate_grads.T, jnp.transpose(share, (1, 0, 2))[None]


def solution(mesh):
    torus = Mesh(mesh.devices.reshape(4, 4, mesh.shape["expert"]), ("dp_0", "dp_1", "expert"))
    in_specs = (
        P(DP_EXPERT, None),
        P(DP_EXPERT, None),
        P(DP_EXPERT, None),
        P(DP_EXPERT, None),
        P(),
        P(),
        P("expert", None, None, None),
    )
    out_specs = (
        P(DP_EXPERT, None),
        P(DP_EXPERT, None),
        P(DP_EXPERT, None),
        P("expert", DP, None, None),
    )
    return jax.shard_map(
        on_device, mesh=torus, in_specs=in_specs, out_specs=out_specs, check_vma=False
    )
```
